256 devices in a mesh: dp: 32 (over z_lo, x, core), grad: 8 (over z_hi, y).
Axes of the slice: x: 4, y: 4, z: 8 (z_hi: 2, z_lo: 4; z = z_hi * 4 + z_lo), core: 2. Of those that a mesh axis runs over, the one named last changes fastest.
Arguments:
- grad_att: bfloat16 [8192, 8192], P('dp', 'grad'), may hold values from -6 to 6
- grad_mlp: bfloat16 [8192, 28672], P('dp', 'grad'), may hold values from -6 to 6
- acts_att: bfloat16 [8192, 8192], P('dp', 'grad'), may hold values from -6 to 6
- acts_mlp: bfloat16 [8192, 28672], P('dp', 'grad'), may hold values from -6 to 6
- basis_in_att: bfloat16 [32, 8192, 512], P('dp', 'grad'), may hold values from -0.25 to 0.25
- basis_in_mlp: bfloat16 [32, 28672, 512], P('dp', 'grad'), may hold values from -0.25 to 0.25
- basis_out_att: bfloat16 [8, 8192, 512], P('grad', 'dp'), may hold values from -0.25 to 0.25
- basis_out_mlp: bfloat16 [8, 8192, 512], P('grad', 'dp'), may hold values from -0.25 to 0.25
- lam_out: float32 [8, 2, 512], P('grad'), may hold values from 0.5 to 5
- owner_dp: int32 [2], replicated, may hold values from 0 to 31
- owner_grad: int32 [2], replicated, may hold values from 0 to 7
Outputs:
- precond_att: bfloat16 [8192, 8192], P('dp', 'grad')
- precond_mlp: bfloat16 [8192, 28672], P('dp', 'grad')
The draws below stay inside these ranges and needn't reach their ends.
All inputs are finite; a program needn't handle non-finite values.
Results may differ from the reference program's by a relative error of at most 0.014.
Values may be sent and summed in bfloat16 or wider, within the bound.
No kernel may reach another device: no remote copies, remote signals or barrier semaphores. Data moves between devices by JAX's collectives and lax.ppermute only.
A program may use at most 64 MiB of HBM per device.

```python
import math
import jax
import jax.numpy as jnp
from jax import lax

OUT = 8192
IN_ATT = 8192
IN_MLP = 28672
K = 512
TOKENS = 8192
N_DP = 32
N_GRAD = 8


def block_scale(key, shape, cuts, low, high):
    def one(axis_at, blocks):
        steps = jax.random.uniform(jax.random.fold_in(jax.random.fold_in(key, 6), axis_at), (blocks,), jnp.float32, low / len(cuts), high / len(cuts))
        return jnp.repeat(jnp.exp(steps), shape[axis_at] // blocks).reshape((-1,) + (1,) * (len(shape) - axis_at - 1))

    loudness = one(*cuts[0])
    for cut in cuts[1:]:
        loudness = loudness * one(*cut)
    return loudness


def centred(stream_key, dims, scale, bound, shards=(), dtype=jnp.bfloat16):
    array = scale * jax.random.normal(stream_key, dims, jnp.float32)
    if shards:
        array = array * block_scale(stream_key, dims, shards, -0.22, 0.18)
    return jnp.clip(array, -bound, bound).astype(dtype)


def setup_inputs(seed: int = 0) -> dict:
    keys = jax.random.split(jax.random.key(seed), 12)
    grad_att = centred(keys[0], (OUT, IN_ATT), 1.0, 6.0, ((0, 32), (1, 8)))
    grad_mlp = centred(keys[1], (OUT, IN_MLP), 1.0, 6.0, ((0, 32), (1, 8)))
    acts_att = centred(keys[2], (TOKENS, IN_ATT), 1.0, 6.0, ((0, 32), (1, 8)))
    acts_mlp = centred(keys[3], (TOKENS, IN_MLP), 1.0, 6.0, ((0, 32), (1, 8)))
    basis_in_att = centred(keys[4], (N_DP, IN_ATT, K), K ** -0.5, 0.25, ((0, 32), (1, 8)))
    basis_in_mlp = centred(keys[5], (N_DP, IN_MLP, K), K ** -0.5, 0.25, ((0, 32), (1, 8)))
    basis_out_att = centred(keys[6], (N_GRAD, OUT, K), K ** -0.5, 0.25, ((0, 8), (1, 32)))
    basis_out_mlp = centred(keys[7], (N_GRAD, OUT, K), K ** -0.5, 0.25, ((0, 8), (1, 32)))
    lam_out = jnp.clip(jnp.exp(math.log(5.0) - 2.3025851 * jax.random.uniform(keys[8], (N_GRAD, 2, K), jnp.float32) ** block_scale(keys[8], (N_GRAD, 2, K), ((0, 8),), -0.2, 0.2)), 0.5, 5.0)
    owner_dp = jax.random.randint(keys[9], (2,), 0, N_DP).astype(jnp.int32)
    owner_grad = jax.random.randint(keys[10], (2,), 0, N_GRAD).astype(jnp.int32)
    return {"grad_att": grad_att, "grad_mlp": grad_mlp, "acts_att": acts_att, "acts_mlp": acts_mlp, "basis_in_att": basis_in_att, "basis_in_mlp": basis_in_mlp, "basis_out_att": basis_out_att, "basis_out_mlp": basis_out_mlp, "lam_out": lam_out, "owner_dp": owner_dp, "owner_grad": owner_grad}


DAMP_REL = 0.1


def one_layer(grads, acts, basis_in_all, basis_out_all, lam_out, owner_in, owner_out, layer):
    basis_in = basis_in_all[owner_in[layer]]
    basis_out = basis_out_all[owner_out[layer]]
    lam_g = lam_out[owner_out[layer], layer]
    projected = jnp.dot(acts, basis_in, preferred_element_type=jnp.float32)
    lam_a = jnp.sum(projected * projected, axis=0) / TOKENS
    damp = DAMP_REL * jnp.mean(lam_g) * jnp.mean(lam_a)
    rotated = jnp.dot(grads, basis_in, preferred_element_type=jnp.float32)
    core = jnp.dot(basis_out.astype(jnp.float32).T, rotated, precision=lax.Precision.HIGHEST)
    scaled = core / (lam_g[:, None] * lam_a[None, :] + damp)
    lifted = jnp.dot(basis_out.astype(jnp.float32), scaled, precision=lax.Precision.HIGHEST).astype(jnp.bfloat16)
    return jnp.dot(lifted, basis_in.T, preferred_element_type=jnp.float32).astype(jnp.bfloat16)


def reference(grad_att, grad_mlp, acts_att, acts_mlp, basis_in_att, basis_in_mlp, basis_out_att, basis_out_mlp, lam_out, owner_dp, owner_grad):
    precond_att = one_layer(grad_att, acts_att, basis_in_att, basis_out_att, lam_out, owner_dp, owner_grad, 0)
    precond_mlp = one_layer(grad_mlp, acts_mlp, basis_in_mlp, basis_out_mlp, lam_out, owner_dp, owner_grad, 1)
    return precond_att, precond_mlp
```

```python
import jax
import jax.numpy as jnp
from jax import lax
from jax.sharding import Mesh, PartitionSpec as P

DAMP_REL = 0.1
AXES = ("z_lo", "x", "core", "z_hi", "y")
SIZES = (4, 4, 2, 2, 4)
SIZE = dict(zip(AXES, SIZES))
DP = ("z_lo", "x", "core")
GRAD = ("z_hi", "y")
BF = jnp.bfloat16
F32 = jnp.float32


def swap(value, axis, k):
    n = SIZE[axis]
    return lax.ppermute(value, axis, [(i, i ^ k) for i in range(n)])


def block(value, index, rows):
    return lax.dynamic_slice_in_dim(value, index * rows, rows, 0)


def scatter_from(value, axis, owner):
    n, me = SIZE[axis], lax.axis_index(axis)
    rows = value.shape[0] // n
    got = block(value, me, rows)
    parts = [swap(block(value, me ^ k, rows), axis, k) for k in range(1, n)]
    for k, part in enumerate(parts, 1):
        got = jnp.where((me ^ k) == owner, part, got)
    return got


def gather(value, axis):
    n, me = SIZE[axis], lax.axis_index(axis)
    rows = value.shape[0]
    parts = [value] + [swap(value, axis, k) for k in range(1, n)]
    out = jnp.zeros((n * rows,) + value.shape[1:], value.dtype)
    for k, part in enumerate(parts):
        out = lax.dynamic_update_slice_in_dim(out, part, (me ^ k) * rows, 0)
    return out


def reduce_scatter(value, axis):
    n, me = SIZE[axis], lax.axis_index(axis)
    rows = value.shape[0] // n
    parts = [swap(block(value, me ^ k, rows).astype(BF), axis, k) for k in range(1, n)]
    total = block(value, me, rows)
    for part in parts:
        total = total + part.astype(F32)
    return total


def all_sum(value, axis):
    n = SIZE[axis]
    sent = value.astype(BF)
    total = value
    for k in range(1, n):
        total = total + swap(sent, axis, k).astype(F32)
    return total


def split3(value):
    a = lax.reduce_precision(value, 8, 7)
    b = lax.reduce_precision(value - a, 8, 7)
    return a.astype(BF), b.astype(BF), (value - a - b).astype(BF)


def broadcast_basis(mine, owner, order):
    core = owner % 2
    at = {"core": core, "x": (owner // 2) % 4, "z_lo": owner // 8}
    value = mine
    for axis in order:
        value = scatter_from(value, axis, at[axis])
    for axis in reversed(order):
        value = gather(value, axis)
    return value


def broadcast_out(basis_att, basis_mlp, lam, owner_grad):
    y, hi = lax.axis_index("y"), lax.axis_index("z_hi")
    halves = []
    for layer, rows in enumerate((basis_att, basis_mlp)):
        eig = split3(lam[layer])
        extra = jnp.concatenate([e[None] for e in eig] + [jnp.zeros((29, 512), BF)], 0)
        halves.append(jnp.concatenate([rows, extra], 0))
    rows = halves[0].shape[0] // 4
    got = []
    for layer in range(2):
        got.append(scatter_from(halves[layer], "y", owner_grad[layer] % 4))
    both = jnp.concatenate(got, 0)
    other = swap(both, "z_hi", 1)
    out = []
    for layer in range(2):
        here = (owner_grad[layer] // 4) == hi
        out.append(jnp.where(here, got[layer], other[layer * rows : (layer + 1) * rows]))
    full = gather(jnp.concatenate(out, 0)[None], "y").reshape(4, 2, rows, 512)
    res = []
    for layer in range(2):
        whole = full[:, layer].reshape(4 * rows, 512)
        lam_g = (
            whole[256].astype(F32) + whole[257].astype(F32) + whole[258].astype(F32)
        )
        res.append((whole[:256], lam_g))
    return res


def one_layer(grads, acts, basis_in, basis_out, lam_g, tokens_all):
    both = jnp.concatenate([grads, acts], 0)
    part = lax.dot_general(basis_in, both, (((0,), (1,)), ((), ())), preferred_element_type=F32)
    part = reduce_scatter(part, "y")
    part = reduce_scatter(part, "z_hi")
    rows = grads.shape[0]
    rot, proj = part[:, :rows], part[:, rows:]
    lam = jnp.sum(proj * proj, axis=1) / tokens_all
    core = jnp.dot(rot, basis_out.astype(F32), precision=lax.Precision.HIGHEST)
    for axis in DP[::-1]:
        core = all_sum(core, axis)
    for axis in DP[::-1]:
        total = lam
        for k in range(1, SIZE[axis]):
            total = total + swap(lam, axis, k)
        lam = total
    a, b, c = split3(lam)
    packed = jnp.concatenate(
        [core.astype(BF), jnp.stack([a, b, c], 1), jnp.zeros((core.shape[0], 125), BF)], 1
    )
    packed = gather(gather(packed, "y"), "z_hi") if False else gather(gather(packed, "z_hi"), "y")
    core = packed[:, :512].astype(F32)
    lam_a = jnp.sum(packed[:, 512:515].astype(F32), axis=1)
    damp = DAMP_REL * jnp.mean(lam_g) * jnp.mean(lam_a)
    scaled = core / (lam_g[None, :] * lam_a[:, None] + damp)
    lifted = lax.dot_general(
        basis_out.astype(F32), scaled, (((1,), (1,)), ((), ())), precision=lax.Precision.HIGHEST
    ).astype(BF)
    return lax.dot_general(
        lifted, basis_in, (((1,), (1,)), ((), ())), preferred_element_type=F32
    ).astype(BF)


def body(
    grad_att,
    grad_mlp,
    acts_att,
    acts_mlp,
    basis_in_att,
    basis_in_mlp,
    basis_out_att,
    basis_out_mlp,
    lam_out,
    owner_dp,
    owner_grad,
):
    tokens_all = acts_att.shape[0] * 32
    in_att = broadcast_basis(basis_in_att[0], owner_dp[0], ("core", "z_lo", "x"))
    in_mlp = broadcast_basis(basis_in_mlp[0], owner_dp[1], ("core", "x", "z_lo"))
    (out_att, g_att), (out_mlp, g_mlp) = broadcast_out(
        basis_out_att[0], basis_out_mlp[0], lam_out[0], owner_grad
    )
    return (
        one_layer(grad_att, acts_att, in_att, out_att, g_att, tokens_all),
        one_layer(grad_mlp, acts_mlp, in_mlp, out_mlp, g_mlp, tokens_all),
    )


def solution(mesh):
    fine = Mesh(mesh.devices.reshape(SIZES), AXES)
    placed = (
        P(DP, GRAD),
        P(DP, GRAD),
        P(DP, GRAD),
        P(DP, GRAD),
        P(DP, GRAD, None),
        P(DP, GRAD, None),
        P(GRAD, DP, None),
        P(GRAD, DP, None),
        P(GRAD, None, None),
        P(),
        P(),
    )
    return jax.shard_map(
        body,
        mesh=fine,
        in_specs=placed,
        out_specs=(P(DP, GRAD), P(DP, GRAD)),
        check_vma=False,
    )
```

```python
import jax
import jax.numpy as jnp
from jax import lax
from jax.sharding import Mesh, PartitionSpec as P

DAMP_REL = 0.1
AXES = ("z_lo", "x", "core", "z_hi", "y")
SIZES = (4, 4, 2, 2, 4)
SIZE = dict(zip(AXES, SIZES))
DP = ("z_lo", "x", "core")
GRAD = ("z_hi", "y")
BF = jnp.bfloat16
F32 = jnp.float32
HIGH = lax.Precision.HIGHEST


def block(value, index, rows, axis=0):
    start = [0] * value.ndim
    start[axis] = index * rows
    size = list(value.shape)
    size[axis] = rows
    return lax.dynamic_slice(value, start, size, allow_negative_indices=False)


def put(value, part, index, axis=0):
    start = [0] * value.ndim
    start[axis] = index * part.shape[axis]
    return lax.dynamic_update_slice(value, part, start, allow_negative_indices=False)


def swap(value, axis, k=1):
    return lax.ppermute(value, axis, [(i, i ^ k) for i in range(SIZE[axis])])


def side(axis, k, pair):
    me = lax.axis_index(axis)
    if pair == (1,):
        return me
    first, second = pair
    if {first, second} == {1, 3}:
        if k == 3:
            return me >> 1
        return (me ^ (me >> 1)) & 1 if first == 1 else me & 1
    return me & 1 if k == 1 else me >> 1


def deal(value, axis, ks, at):
    me = lax.axis_index(axis)
    kept = []
    for k in ks:
        mine, rows = side(axis, k, ks), value.shape[1] // 2
        got = swap(block(value, 1 - mine, rows, 1), axis, k)
        own = me == at
        for j in kept:
            own = own | ((me ^ j) == at)
        own = own.reshape((-1,) + (1,) * (value.ndim - 1))
        value = jnp.where(own, block(value, mine, rows, 1), got)
        kept.append(k)
    return value


def gather(value, axis, ks):
    for k in ks[::-1]:
        mine = side(axis, k, ks)
        twice = jnp.concatenate([value, value], 1)
        value = put(twice, swap(value, axis, k), 1 - mine, 1)
    return value


def split2(value):
    a = lax.reduce_precision(value, 8, 7)
    return a, lax.reduce_precision(value - a, 8, 7)


def split3(value):
    a, b = split2(value)
    return [a.astype(BF), b.astype(BF), (value - a - b).astype(BF)]


def packed(core, lam):
    a, b = split2(lam)
    lane = lax.broadcasted_iota(jnp.int32, (core.shape[0], 128), 1)
    more = jnp.where(lane == 0, a, jnp.where(lane == 1, b, 0.0))
    return jnp.concatenate([core.astype(BF), more.astype(BF)], 1)


def unpacked(value):
    wide = value.astype(F32)
    return wide[:, :512], jnp.sum(wide[:, 512:], axis=1, keepdims=True)


def matmul_t(a, b, precision=None):
    return lax.dot_general(
        a, b, (((1,), (1,)), ((), ())), precision=precision, preferred_element_type=F32
    )


RING, RING_B = (1, 3), (3, 1)
LINE, LINE_B = (1, 2), (2, 1)
STREAMS = (
    ((4 + 2, 4 + 8), (), (("x", RING), ("z_lo", LINE))),
    ((4 + 8, 4 + 14), (), (("x", RING_B), ("z_lo", LINE_B))),
    ((4, 5), (0, 2), (("z_lo", LINE), ("x", RING))),
    ((5, 6), (2, 4), (("z_lo", LINE_B), ("x", RING_B))),
)


def broadcast_in(att, mlp, owner):
    wide = att.shape[1]
    na, nm = att.shape[0] // 256, mlp.shape[0] // 256
    whole = jnp.concatenate([att.reshape(2, na, 128, wide), mlp.reshape(2, nm, 128, wide)], 1)
    layer = jnp.array([0] * na + [1] * nm, jnp.int32)
    at = jnp.where(layer == 0, owner[0], owner[1])
    me = lax.axis_index("core")
    got = swap(block(whole, 1 - me, 1)[0], "core")
    own = (me == (at & 1)).reshape(-1, 1, 1)
    value = jnp.where(own, block(whole, me, 1)[0], got)
    full_att = jnp.zeros((2, na, 128, wide), BF)
    full_mlp = jnp.zeros((2, nm, 128, wide), BF)
    for (m0, m1), a, order in STREAMS:
        v, t = value[m0:m1], at[m0:m1]
        if a:
            v = jnp.concatenate([value[a[0] : a[1]], v], 0)
            t = jnp.concatenate([at[a[0] : a[1]], t], 0)
        where = {"x": (t >> 1) & 3, "z_lo": t >> 3}
        for axis, ks in order:
            v = deal(v, axis, ks, where[axis])
        for axis, ks in order[::-1]:
            v = gather(v, axis, ks)
        for w, c in ((v, me), (swap(v, "core"), 1 - me)):
            k = a[1] - a[0] if a else 0
            if a:
                full_att = lax.dynamic_update_slice(
                    full_att, w[None, :k], (c, a[0], 0, 0), allow_negative_indices=False
                )
            full_mlp = lax.dynamic_update_slice(
                full_mlp, w[None, k:], (c, m0 - na, 0, 0), allow_negative_indices=False
            )
    return full_att.reshape(att.shape), full_mlp.reshape(mlp.shape)


def broadcast_out(att, mlp, lam, owner):
    rows = att.shape[0]
    both = jnp.stack(
        [
            jnp.concatenate([b, jnp.stack(split3(lam[l])), jnp.zeros((29, b.shape[1]), BF)], 0)
            for l, b in enumerate((att, mlp))
        ]
    )
    both = deal(both, "y", RING, owner & 3)
    here = (lax.axis_index("z_hi") == (owner >> 2)).reshape(2, 1, 1)
    both = jnp.where(here, both, swap(both, "z_hi"))
    both = gather(both, "y", RING)
    return both[:, :rows].astype(F32), jnp.sum(both[:, rows : rows + 3].astype(F32), axis=1)


def reduce_scatter(value, axis):
    n, me = SIZE[axis], lax.axis_index(axis)
    rows = value.shape[0] // n
    got = [swap(block(value, me ^ k, rows).astype(BF), axis, k) for k in range(1, n)]
    return sum([g.astype(F32) for g in got], block(value, me, rows))


def stack(value, axis):
    n, me = SIZE[axis], lax.axis_index(axis)
    out = jnp.stack([value] * n)
    for k in range(1, n):
        out = put(out, swap(value, axis, k)[None], me ^ k)
    return out


def body(
    grad_att,
    grad_mlp,
    acts_att,
    acts_mlp,
    basis_in_att,
    basis_in_mlp,
    basis_out_att,
    basis_out_mlp,
    lam_out,
    owner_dp,
    owner_grad,
):
    rows = grad_att.shape[0]
    tokens_all = rows * 32
    basis_out, lam_g = broadcast_out(basis_out_att[0], basis_out_mlp[0], lam_out[0], owner_grad)
    att, mlp = broadcast_in(basis_in_att[0], basis_in_mlp[0], owner_dp)

    part = jnp.concatenate(
        [matmul_t(b.T, v) for b, v in ((att, grad_att), (att, acts_att), (mlp, grad_mlp), (mlp, acts_mlp))],
        1,
    )
    part = reduce_scatter(reduce_scatter(part, "y"), "z_hi")

    mine = []
    for l in range(2):
        rot = part[:, 2 * l * rows : (2 * l + 1) * rows]
        proj = part[:, (2 * l + 1) * rows : (2 * l + 2) * rows]
        lam = jnp.sum(proj * proj, axis=1, keepdims=True) / tokens_all
        mine.append((jnp.dot(rot, basis_out[l], precision=HIGH), lam))
    half = part.shape[0] // 2
    me = lax.axis_index("core")
    core = jnp.concatenate([block(c, me, half) for c, _ in mine], 0)
    lam = jnp.concatenate([block(e, me, half) for _, e in mine], 0)
    sent = packed(
        jnp.concatenate([block(c, 1 - me, half) for c, _ in mine], 0),
        jnp.concatenate([block(e, 1 - me, half) for _, e in mine], 0),
    )
    c, e = unpacked(swap(sent, "core"))
    core, lam = core + c, lam + e
    for axis in ("x", "z_lo"):
        sent = packed(core, lam)
        for v in [swap(sent, axis, k) for k in (1, 2, 3)]:
            c, e = unpacked(v)
            core, lam = core + c, lam + e

    wide = packed(core, lam).reshape(2, half, 640)
    wide = stack(stack(stack(wide, "z_hi"), "y"), "core")
    wide = wide.transpose(3, 1, 2, 0, 4, 5).reshape(2, 512, 640)
    res = []
    for l, basis in enumerate((att, mlp)):
        core, lam_a = unpacked(wide[l])
        damp = DAMP_REL * jnp.mean(lam_g[l]) * jnp.mean(lam_a)
        scaled = core / (lam_g[l][None, :] * lam_a + damp)
        lifted = matmul_t(basis_out[l], scaled, HIGH).astype(BF)
        res.append(matmul_t(lifted, basis).astype(BF))
    return tuple(res)


def solution(mesh):
    fine = Mesh(mesh.devices.reshape(SIZES), AXES)
    placed = (
        P(DP, GRAD),
        P(DP, GRAD),
        P(DP, GRAD),
        P(DP, GRAD),
        P(DP, GRAD, None),
        P(DP, GRAD, None),
        P(GRAD, DP, None),
        P(GRAD, DP, None),
        P(GRAD, None, None),
        P(),
        P(),
    )
    return jax.shard_map(
        body,
        mesh=fine,
        in_specs=placed,
        out_specs=(P(DP, GRAD), P(DP, GRAD)),
        check_vma=False,
    )
```

```python
import jax
import jax.numpy as jnp
from jax import lax
from jax.sharding import Mesh, PartitionSpec as P

DAMP_REL = 0.1
AXES = ("z_lo", "x", "core", "z_hi", "y")
SIZES = (4, 4, 2, 2, 4)
SIZE = dict(zip(AXES, SIZES))
DP = ("z_lo", "x", "core")
GRAD = ("z_hi", "y")
BF = jnp.bfloat16
F32 = jnp.float32


def block(value, index, rows, axis=0):
    start = [0] * value.ndim
    start[axis] = index * rows
    size = list(value.shape)
    size[axis] = rows
    return lax.dynamic_slice(value, start, size, allow_negative_indices=False)


def put(value, part, index, axis=0):
    start = [0] * value.ndim
    start[axis] = index * part.shape[axis]
    return lax.dynamic_update_slice(value, part, start, allow_negative_indices=False)


def swap(value, axis, k=1):
    return lax.ppermute(value, axis, [(i, i ^ k) for i in range(SIZE[axis])])


def side(axis, k, pair):
    me = lax.axis_index(axis)
    if pair == (1,):
        return me
    first, second = pair
    if {first, second} == {1, 3}:
        if k == 3:
            return me >> 1
        return (me ^ (me >> 1)) & 1 if first == 1 else me & 1
    return me & 1 if k == 1 else me >> 1


def half_out(value, axis, k, pair):
    return block(value, 1 - side(axis, k, pair), value.shape[1] // 2, 1)


def half_in(value, got, axis, k, pair, at):
    me = lax.axis_index(axis)
    own = me == at
    if k == pair[-1] and len(pair) == 2:
        own = own | ((me ^ pair[0]) == at)
    if own.ndim:
        own = own.reshape((-1,) + (1,) * (value.ndim - 1))
    return jnp.where(own, block(value, side(axis, k, pair), value.shape[1] // 2, 1), got)


def join(value, got, axis, k, pair):
    return put(jnp.concatenate([value, value], 1), got, 1 - side(axis, k, pair), 1)


def parts_out(value, axis, dim):
    me, rows = lax.axis_index(axis), value.shape[dim] // SIZE[axis]
    return [block(value, me ^ k, rows, dim) for k in range(1, SIZE[axis])]


def part_in(value, got, axis, dim, at):
    me = lax.axis_index(axis)
    mine = block(value, me, value.shape[dim] // SIZE[axis], dim)
    for k, g in enumerate(got, 1):
        mine = jnp.where((me ^ k) == at, g, mine)
    return mine


def parts_join(value, got, axis, dim):
    me = lax.axis_index(axis)
    out = jnp.concatenate([value] * SIZE[axis], dim)
    for k, g in enumerate(got, 1):
        out = put(out, g, me ^ k, dim)
    return out


def start(*jobs, after=()):
    flat = []
    for job in jobs:
        if len(job) == 2:
            flat += [(v, job[0], k) for k, v in enumerate(job[1], 1)]
        else:
            flat.append((job[2], job[0], job[1]))
    held = lax.optimization_barrier(tuple(f[0] for f in flat) + tuple(after))
    got = [swap(h, axis, k) for h, (_, axis, k) in zip(held, flat)]
    out = []
    for job in jobs:
        n = len(job[1]) if len(job) == 2 else 1
        out.append(got[:n] if len(job) == 2 else got[0])
        got = got[n:]
    return out


def split2(value):
    a = lax.reduce_precision(value, 8, 7)
    return a, lax.reduce_precision(value - a, 8, 7)


def split3(value):
    a, b = split2(value)
    return [a.astype(BF), b.astype(BF), (value - a - b).astype(BF)]


def packed(core, lam):
    a, b = split2(lam)
    lane = lax.broadcasted_iota(jnp.int32, (core.shape[0], 128), 1)
    more = jnp.where(lane == 0, a, jnp.where(lane == 1, b, 0.0))
    return jnp.concatenate([core.astype(BF), more.astype(BF)], 1)


def unpacked(value):
    wide = value.astype(F32)
    return wide[:, :512], jnp.sum(wide[:, 512:], axis=1, keepdims=True)


def matmul_t(a, b):
    return lax.dot_general(a, b, (((1,), (1,)), ((), ())), preferred_element_type=F32)


RING, RING_B = (1, 3), (3, 1)
LINE, LINE_B = (1, 2), (2, 1)


class Tail:
    def __init__(self, basis, grads, acts, tokens_all):
        self.rows, self.tokens_all = grads.shape[0], tokens_all
        self.part = jnp.concatenate([matmul_t(basis.T, grads), matmul_t(basis.T, acts)], 1)

    def sum_out(self, axis):
        return axis, [v.astype(BF) for v in parts_out(self.part, axis, 0)]

    def sum_in(self, got, axis):
        mine = block(self.part, lax.axis_index(axis), self.part.shape[0] // SIZE[axis])
        self.part = sum([g.astype(F32) for g in got], mine)

    def core_out(self, basis_out):
        rot, proj = self.part[:, : self.rows], self.part[:, self.rows :]
        lam = jnp.sum(proj * proj, axis=1, keepdims=True) / self.tokens_all
        n = rot.shape[0]
        both = jnp.dot(
            jnp.concatenate([v.astype(BF) for v in split2(rot)], 0),
            basis_out,
            preferred_element_type=F32,
        )
        core = both[:n] + both[n:]
        me, half = lax.axis_index("core"), n // 2
        self.core, self.lam = block(core, me, half), block(lam, me, half)
        return "core", 1, packed(block(core, 1 - me, half), block(lam, 1 - me, half))

    def add(self, got):
        for v in got:
            c, e = unpacked(v)
            self.core, self.lam = self.core + c, self.lam + e

    def all_out(self, axis):
        return axis, [packed(self.core, self.lam)] * 3

    def first_out(self):
        self.wide = packed(self.core, self.lam)[None, None]
        return "z_hi", [self.wide]

    def gather_out(self, got, last, axis):
        dim = {"z_hi": 1, "y": 0}[last]
        self.wide = parts_join(self.wide, got, last, dim)
        return axis, [self.wide] * (SIZE[axis] - 1)

    def finish(self, got, basis, basis_out, lam_g):
        me = lax.axis_index("core")
        wide = jnp.stack([self.wide] * 2, 2)
        wide = put(wide, got[0][:, :, None], 1 - me, 2).reshape(512, 640)
        core, lam_a = unpacked(wide)
        damp = DAMP_REL * jnp.mean(lam_g) * jnp.mean(lam_a)
        scaled = core / (lam_g[None, :] * lam_a + damp)
        a, b = split2(scaled)
        lifted = (matmul_t(basis_out, a.astype(BF)) + matmul_t(basis_out, b.astype(BF))).astype(BF)
        return matmul_t(lifted, basis).astype(BF)


def body(
    grad_att,
    grad_mlp,
    acts_att,
    acts_mlp,
    basis_in_att,
    basis_in_mlp,
    basis_out_att,
    basis_out_mlp,
    lam_out,
    owner_dp,
    owner_grad,
):
    rows = grad_att.shape[0]
    tokens_all = rows * 32
    c = lax.axis_index("core")
    at_c, at_x, at_z = owner_dp & 1, (owner_dp >> 1) & 3, owner_dp >> 3
    x1, z1 = at_x[1], at_z[1]

    att = basis_in_att.reshape(2, -1, 4, 4, 8, 512)
    mlp = basis_in_mlp.reshape(2, -1, 128, 512)
    out = jnp.stack(
        [
            jnp.concatenate(
                [v[0], jnp.stack(split3(lam_out[0, l])), jnp.zeros((29, 512), BF)], 0
            )
            for l, v in enumerate((basis_out_att, basis_out_mlp))
        ]
    )

    g_att, g_mlp, g_out = start(
        ("core", 1, block(att, 1 - c, 1)[0]),
        ("core", 1, block(mlp, 1 - c, 1)[0]),
        ("y", 1, half_out(out, "y", 1, RING)),
    )
    att = jnp.where(c == at_c[0], block(att, c, 1)[0], g_att)
    mlp = jnp.where(c == at_c[1], block(mlp, c, 1)[0], g_mlp)
    half = mlp.shape[0] // 2
    a, b = mlp[:half], mlp[half:]

    ga, gb, gt = start(
        ("x", 1, half_out(a, "x", 1, RING)),
        ("x", 3, half_out(b, "x", 3, RING_B)),
        ("z_lo", parts_out(att, "z_lo", 1)),
        after=(g_out,),
    )
    att = part_in(att, gt, "z_lo", 1, at_z[0])
    (gt,) = start(("x", parts_out(att, "x", 2)))
    att = part_in(att, gt, "x", 2, at_x[0])
    a, b = half_in(a, ga, "x", 1, RING, x1), half_in(b, gb, "x", 3, RING_B, x1)
    ga, gb, gt = start(
        ("x", 3, half_out(a, "x", 3, RING)),
        ("x", 1, half_out(b, "x", 1, RING_B)),
        ("z_lo", [att] * 3),
    )
    att = parts_join(att, gt, "z_lo", 1)
    (gt,) = start(("x", [att] * 3))
    att = parts_join(att, gt, "x", 2)
    a, b = half_in(a, ga, "x", 3, RING, x1), half_in(b, gb, "x", 1, RING_B, x1)

    out = half_in(out, g_out, "y", 1, RING, owner_grad & 3)
    ga, gb, gt, g_out = start(
        ("z_lo", 1, half_out(a, "z_lo", 1, LINE)),
        ("z_lo", 2, half_out(b, "z_lo", 2, LINE_B)),
        ("core", 1, att),
        ("y", 3, half_out(out, "y", 3, RING)),
    )
    att = put(jnp.stack([att, att]), gt[None], 1 - c).reshape(-1, 512)
    out = half_in(out, g_out, "y", 3, RING, owner_grad & 3)
    a, b = half_in(a, ga, "z_lo", 1, LINE, z1), half_in(b, gb, "z_lo", 2, LINE_B, z1)
    ga, gb, g_out = start(
        ("z_lo", 2, half_out(a, "z_lo", 2, LINE)),
        ("z_lo", 1, half_out(b, "z_lo", 1, LINE_B)),
        ("z_hi", 1, out),
        after=(att,),
    )
    ta = Tail(att, grad_att, acts_att, tokens_all)
    here = (lax.axis_index("z_hi") == (owner_grad >> 2)).reshape(2, 1, 1)
    out = jnp.where(here, out, g_out)
    a, b = half_in(a, ga, "z_lo", 2, LINE, z1), half_in(b, gb, "z_lo", 1, LINE_B, z1)

    ga, gb, gt = start(("z_lo", 2, a), ("z_lo", 1, b), ta.sum_out("y"), after=(out,))
    ta.sum_in(gt, "y")
    a, b = join(a, ga, "z_lo", 2, LINE), join(b, gb, "z_lo", 1, LINE_B)
    ga, gb, gt, g_out = start(
        ("z_lo", 1, a), ("z_lo", 2, b), ta.sum_out("z_hi"), ("y", 3, out)
    )
    ta.sum_in(gt, "z_hi")
    out = join(out, g_out, "y", 3, RING)
    a, b = join(a, ga, "z_lo", 1, LINE), join(b, gb, "z_lo", 2, LINE_B)
    ga, gb, g_out = start(("x", 3, a), ("x", 1, b), ("y", 1, out), after=(ta.part,))
    out = join(out, g_out, "y", 1, RING)
    basis_out = out[:, :rows]
    lam_g = jnp.sum(out[:, rows : rows + 3].astype(F32), axis=1)
    (gt,) = start(ta.core_out(basis_out[0]))
    ta.add([gt])
    a, b = join(a, ga, "x", 3, RING), join(b, gb, "x", 1, RING_B)
    ga, gb, gt = start(("x", 1, a), ("x", 3, b), ta.all_out("x"))
    ta.add(gt)
    (gt,) = start(ta.all_out("z_lo"))
    ta.add(gt)
    a, b = join(a, ga, "x", 1, RING), join(b, gb, "x", 3, RING_B)
    mlp = jnp.concatenate([a, b], 0)

    g_mlp, gt = start(("core", 1, mlp), ta.first_out())
    mlp = put(jnp.stack([mlp, mlp]), g_mlp[None], 1 - c).reshape(-1, 512)
    (gt,) = start(ta.gather_out(gt, "z_hi", "y"))
    tm = Tail(mlp, grad_mlp, acts_mlp, tokens_all)
    gm, gt = start(tm.sum_out("y"), ta.gather_out(gt, "y", "core"))
    tm.sum_in(gm, "y")
    (gm,) = start(tm.sum_out("z_hi"), after=gt)
    precond_att = ta.finish(gt, att, basis_out[0], lam_g[0])
    tm.sum_in(gm, "z_hi")
    (gm,) = start(tm.core_out(basis_out[1]), after=(precond_att,))
    tm.add([gm])
    (gm,) = start(tm.all_out("x"))
    tm.add(gm)
    (gm,) = start(tm.all_out("z_lo"))
    tm.add(gm)
    (gm,) = start(tm.first_out())
    (gm,) = start(tm.gather_out(gm, "z_hi", "y"))
    (gm,) = start(tm.gather_out(gm, "y", "core"))
    return precond_att, tm.finish(gm, mlp, basis_out[1], lam_g[1])


def solution(mesh):
    fine = Mesh(mesh.devices.reshape(SIZES), AXES)
    placed = (
        P(DP, GRAD),
        P(DP, GRAD),
        P(DP, GRAD),
        P(DP, GRAD),
        P(DP, GRAD, None),
        P(DP, GRAD, None),
        P(GRAD, DP, None),
        P(GRAD, DP, None),
        P(GRAD, None, None),
        P(),
        P(),
    )
    return jax.shard_map(
        body,
        mesh=fine,
        in_specs=placed,
        out_specs=(P(DP, GRAD), P(DP, GRAD)),
        check_vma=False,
    )
```

```python
import jax
import jax.numpy as jnp
from jax import lax
from jax.sharding import Mesh, PartitionSpec as P

DAMP_REL = 0.1
AXES = ("z_lo", "x", "core", "z_hi", "y")
SIZES = (4, 4, 2, 2, 4)
SIZE = dict(zip(AXES, SIZES))
DP = ("z_lo", "x", "core")
GRAD = ("z_hi", "y")
BF = jnp.bfloat16
F32 = jnp.float32


def block(value, index, rows, axis=0):
    start = [0] * value.ndim
    start[axis] = index * rows
    size = list(value.shape)
    size[axis] = rows
    return lax.dynamic_slice(value, start, size, allow_negative_indices=False)


def put(value, part, index, axis=0):
    start = [0] * value.ndim
    start[axis] = index * part.shape[axis]
    return lax.dynamic_update_slice(value, part, start, allow_negative_indices=False)


def swap(value, axis, k=1):
    return lax.ppermute(value, axis, [(i, i ^ k) for i in range(SIZE[axis])])


def side(axis, k, pair):
    me = lax.axis_index(axis)
    if pair == (1,):
        return me
    first, second = pair
    if {first, second} == {1, 3}:
        if k == 3:
            return me >> 1
        return (me ^ (me >> 1)) & 1 if first == 1 else me & 1
    return me & 1 if k == 1 else me >> 1


def half_out(value, axis, k, pair):
    return block(value, 1 - side(axis, k, pair), value.shape[1] // 2, 1)


def half_in(value, got, axis, k, pair, at):
    me = lax.axis_index(axis)
    own = me == at
    if k == pair[-1]:
        own = own | ((me ^ pair[0]) == at)
    own = own.reshape((-1,) + (1,) * (value.ndim - 1))
    return jnp.where(own, block(value, side(axis, k, pair), value.shape[1] // 2, 1), got)


def join(value, got, axis, k, pair):
    return put(jnp.concatenate([value, value], 1), got, 1 - side(axis, k, pair), 1)


def start(*jobs):
    held = lax.optimization_barrier(tuple(job[0] for job in jobs))
    return [swap(h, axis, k) for h, (_, axis, k) in zip(held, jobs)]


def split2(value):
    a = lax.reduce_precision(value, 8, 7)
    return a, lax.reduce_precision(value - a, 8, 7)


def split3(value):
    a, b = split2(value)
    return [a.astype(BF), b.astype(BF), (value - a - b).astype(BF)]


def packed(core, lam):
    a, b = split2(lam)
    lane = lax.broadcasted_iota(jnp.int32, (core.shape[0], 128), 1)
    more = jnp.where(lane == 0, a, jnp.where(lane == 1, b, 0.0))
    return jnp.concatenate([core.astype(BF), more.astype(BF)], 1)


def unpacked(value):
    wide = value.astype(F32)
    return wide[:, :512], jnp.sum(wide[:, 512:], axis=1, keepdims=True)


def matmul_t(a, b):
    return lax.dot_general(a, b, (((1,), (1,)), ((), ())), preferred_element_type=F32)


RING, RING_B = (1, 3), (3, 1)
LINE, LINE_B = (1, 2), (2, 1)
STREAMS = (
    ((4 + 2, 4 + 8), (), (("x", RING), ("z_lo", LINE))),
    ((4 + 8, 4 + 14), (), (("x", RING_B), ("z_lo", LINE_B))),
    ((4, 5), (0, 2), (("z_lo", LINE), ("x", RING))),
    ((5, 6), (2, 4), (("z_lo", LINE_B), ("x", RING_B))),
)


def broadcast(att, mlp, owner, out, owner_out):
    wide = att.shape[1]
    na, nm = att.shape[0] // 256, mlp.shape[0] // 256
    whole = jnp.concatenate([att.reshape(2, na, 128, wide), mlp.reshape(2, nm, 128, wide)], 1)
    at = jnp.concatenate([jnp.broadcast_to(owner[0], na), jnp.broadcast_to(owner[1], nm)])
    me = lax.axis_index("core")
    (got,) = start((block(whole, 1 - me, 1)[0], "core", 1))
    own = (me == (at & 1)).reshape(-1, 1, 1)
    value = jnp.where(own, block(whole, me, 1)[0], got)

    def cut(v, blocks, more):
        v = v[blocks[0] : blocks[1]]
        return jnp.concatenate([value[more[0] : more[1]], v], 0) if more else v

    values = [cut(value, m, a) for m, a, _ in STREAMS]
    owners = [
        jnp.concatenate([at[a[0] : a[1]], at[m[0] : m[1]]]) if a else at[m[0] : m[1]]
        for m, a, _ in STREAMS
    ]
    steps = [[(axis, k, ks) for axis, ks in order for k in ks] for _, _, order in STREAMS]
    for n in range(4):
        jobs = [(half_out(v, *st[n]), st[n][0], st[n][1]) for v, st in zip(values, steps)]
        if n < 2:
            jobs.append((half_out(out, "y", RING[n], RING), "y", RING[n]))
        got = start(*jobs)
        values = [
            half_in(v, g, *st[n], (t >> 1) & 3 if st[n][0] == "x" else t >> 3)
            for v, g, st, t in zip(values, got, steps, owners)
        ]
        if n < 2:
            out = half_in(out, got[4], "y", RING[n], RING, owner_out & 3)
    for n in (3, 2, 1, 0):
        jobs = [(v, st[n][0], st[n][1]) for v, st in zip(values, steps)]
        if n == 3:
            jobs.append((out, "z_hi", 1))
        if n < 2:
            jobs.append((out, "y", RING[n]))
        got = start(*jobs)
        values = [join(v, g, *st[n]) for v, g, st in zip(values, got, steps)]
        if n == 3:
            here = (lax.axis_index("z_hi") == (owner_out >> 2)).reshape(2, 1, 1)
            out = jnp.where(here, out, got[4])
        if n < 2:
            out = join(out, got[4], "y", RING[n], RING)
    got = start(*[(v, "core", 1) for v in values])
    full_att = [jnp.concatenate([v[2][:2], v[3][:2]], 0) for v in (values, got)]
    full_mlp = [
        jnp.concatenate([v[2][2:], v[3][2:], v[0], v[1]], 0) for v in (values, got)
    ]

    def whole_of(mine, other):
        return put(jnp.stack([mine, mine]), other[None], 1 - me)

    return whole_of(*full_att).reshape(att.shape), whole_of(*full_mlp).reshape(mlp.shape), out


def reduce_scatter(value, axis):
    n, me = SIZE[axis], lax.axis_index(axis)
    rows = value.shape[0] // n
    got = [swap(block(value, me ^ k, rows).astype(BF), axis, k) for k in range(1, n)]
    return sum([g.astype(F32) for g in got], block(value, me, rows))


def stack(value, axis):
    n, me = SIZE[axis], lax.axis_index(axis)
    out = jnp.stack([value] * n)
    for k in range(1, n):
        out = put(out, swap(value, axis, k)[None], me ^ k)
    return out


def body(
    grad_att,
    grad_mlp,
    acts_att,
    acts_mlp,
    basis_in_att,
    basis_in_mlp,
    basis_out_att,
    basis_out_mlp,
    lam_out,
    owner_dp,
    owner_grad,
):
    rows = grad_att.shape[0]
    tokens_all = rows * 32
    out = jnp.stack(
        [
            jnp.concatenate(
                [v[0], jnp.stack(split3(lam_out[0, l])), jnp.zeros((29, 512), BF)], 0
            )
            for l, v in enumerate((basis_out_att, basis_out_mlp))
        ]
    )
    att, mlp, out = broadcast(basis_in_att[0], basis_in_mlp[0], owner_dp, out, owner_grad)
    basis_out = out[:, :rows]
    lam_g = jnp.sum(out[:, rows : rows + 3].astype(F32), axis=1)

    part = jnp.concatenate(
        [matmul_t(b.T, v) for b, v in ((att, grad_att), (att, acts_att), (mlp, grad_mlp), (mlp, acts_mlp))],
        1,
    )
    part = reduce_scatter(reduce_scatter(part, "y"), "z_hi")

    mine = []
    for l in range(2):
        rot = part[:, 2 * l * rows : (2 * l + 1) * rows]
        proj = part[:, (2 * l + 1) * rows : (2 * l + 2) * rows]
        lam = jnp.sum(proj * proj, axis=1, keepdims=True) / tokens_all
        both = jnp.concatenate([v.astype(BF) for v in split2(rot)], 0)
        both = jnp.dot(both, basis_out[l], preferred_element_type=F32)
        n = rot.shape[0]
        mine.append((both[:n] + both[n:], lam))
    half = part.shape[0] // 2
    me = lax.axis_index("core")
    core = jnp.concatenate([block(c, me, half) for c, _ in mine], 0)
    lam = jnp.concatenate([block(e, me, half) for _, e in mine], 0)
    sent = packed(
        jnp.concatenate([block(c, 1 - me, half) for c, _ in mine], 0),
        jnp.concatenate([block(e, 1 - me, half) for _, e in mine], 0),
    )
    c, e = unpacked(swap(sent, "core"))
    core, lam = core + c, lam + e
    for axis in ("x", "z_lo"):
        sent = packed(core, lam)
        for v in [swap(sent, axis, k) for k in (1, 2, 3)]:
            c, e = unpacked(v)
            core, lam = core + c, lam + e

    wide = packed(core, lam).reshape(2, half, 640)
    wide = stack(stack(stack(wide, "z_hi"), "y"), "core")
    wide = wide.transpose(3, 1, 2, 0, 4, 5).reshape(2, 512, 640)
    res = []
    for l, basis in enumerate((att, mlp)):
        core, lam_a = unpacked(wide[l])
        damp = DAMP_REL * jnp.mean(lam_g[l]) * jnp.mean(lam_a)
        scaled = core / (lam_g[l][None, :] * lam_a + damp)
        a, b = split2(scaled)
        lifted = matmul_t(basis_out[l], a.astype(BF)) + matmul_t(basis_out[l], b.astype(BF))
        lifted = lifted.astype(BF)
        res.append(matmul_t(lifted, basis).astype(BF))
    return tuple(res)


def solution(mesh):
    fine = Mesh(mesh.devices.reshape(SIZES), AXES)
    placed = (
        P(DP, GRAD),
        P(DP, GRAD),
        P(DP, GRAD),
        P(DP, GRAD),
        P(DP, GRAD, None),
        P(DP, GRAD, None),
        P(GRAD, DP, None),
        P(GRAD, DP, None),
        P(GRAD, None, None),
        P(),
        P(),
    )
    return jax.shard_map(
        body,
        mesh=fine,
        in_specs=placed,
        out_specs=(P(DP, GRAD), P(DP, GRAD)),
        check_vma=False,
    )
```

```python
import functools

import jax
import jax.numpy as jnp
from jax import lax
from jax.experimental import pallas as pl
from jax.experimental.pallas import tpu as pltpu
from jax.sharding import Mesh, PartitionSpec as P

DAMP_REL = 0.1
AXES = ("z_lo", "x", "core", "z_hi", "y")
SIZES = (4, 4, 2, 2, 4)
SIZE = dict(zip(AXES, SIZES))
DP = ("z_lo", "x", "core")
GRAD = ("z_hi", "y")
BF = jnp.bfloat16
F32 = jnp.float32


def block(value, index, rows, axis=0):
    start = [0] * value.ndim
    start[axis] = index * rows
    size = list(value.shape)
    size[axis] = rows
    return lax.dynamic_slice(value, start, size, allow_negative_indices=False)


def put(value, part, index, axis=0):
    start = [0] * value.ndim
    start[axis] = index * part.shape[axis]
    return lax.dynamic_update_slice(value, part, start, allow_negative_indices=False)


def swap(value, axis, k=1):
    return lax.ppermute(value, axis, [(i, i ^ k) for i in range(SIZE[axis])])


def side(axis, k, pair):
    me = lax.axis_index(axis)
    if pair == (1,):
        return me
    first, second = pair
    if {first, second} == {1, 3}:
        if k == 3:
            return me >> 1
        return (me ^ (me >> 1)) & 1 if first == 1 else me & 1
    return me & 1 if k == 1 else me >> 1


def half_out(value, axis, k, pair):
    return block(value, 1 - side(axis, k, pair), value.shape[1] // 2, 1)


def half_in(value, got, axis, k, pair, at):
    me = lax.axis_index(axis)
    own = me == at
    if k == pair[-1]:
        own = own | ((me ^ pair[0]) == at)
    own = own.reshape((-1,) + (1,) * (value.ndim - 1))
    return jnp.where(own, block(value, side(axis, k, pair), value.shape[1] // 2, 1), got)


def join(value, got, axis, k, pair):
    return put(jnp.concatenate([value, value], 1), got, 1 - side(axis, k, pair), 1)


def start(*jobs):
    held = lax.optimization_barrier(tuple(job[0] for job in jobs))
    return [swap(h, axis, k) for h, (_, axis, k) in zip(held, jobs)]


def split2(value):
    a = lax.reduce_precision(value, 8, 7)
    return a, lax.reduce_precision(value - a, 8, 7)


def split3(value):
    a, b = split2(value)
    return [a.astype(BF), b.astype(BF), (value - a - b).astype(BF)]


def packed(core, lam):
    a, b = split2(lam)
    lane = lax.broadcasted_iota(jnp.int32, (core.shape[0], 128), 1)
    more = jnp.where(lane == 0, a, jnp.where(lane == 1, b, 0.0))
    return jnp.concatenate([core.astype(BF), more.astype(BF)], 1)


def unpacked(value):
    wide = value.astype(F32)
    return wide[:, :512], jnp.sum(wide[:, 512:], axis=1, keepdims=True)


def matmul_t(a, b):
    return lax.dot_general(a, b, (((1,), (1,)), ((), ())), preferred_element_type=F32)


RING, RING_B = (1, 3), (3, 1)
LINE, LINE_B = (1, 2), (2, 1)
STREAMS = (
    ((4 + 2, 4 + 8), (), (("x", RING), ("z_lo", LINE))),
    ((4 + 8, 4 + 14), (), (("x", RING_B), ("z_lo", LINE_B))),
    ((4, 5), (0, 2), (("z_lo", LINE), ("x", RING))),
    ((5, 6), (2, 4), (("z_lo", LINE_B), ("x", RING_B))),
)


def broadcast(att, mlp, owner, out, owner_out):
    wide = att.shape[1]
    na, nm = att.shape[0] // 256, mlp.shape[0] // 256
    whole = jnp.concatenate([att.reshape(2, na, 128, wide), mlp.reshape(2, nm, 128, wide)], 1)
    at = jnp.concatenate([jnp.broadcast_to(owner[0], na), jnp.broadcast_to(owner[1], nm)])
    me = lax.axis_index("core")
    (got,) = start((block(whole, 1 - me, 1)[0], "core", 1))
    own = (me == (at & 1)).reshape(-1, 1, 1)
    value = jnp.where(own, block(whole, me, 1)[0], got)

    def cut(v, blocks, more):
        v = v[blocks[0] : blocks[1]]
        return jnp.concatenate([value[more[0] : more[1]], v], 0) if more else v

    values = [cut(value, m, a) for m, a, _ in STREAMS]
    owners = [
        jnp.concatenate([at[a[0] : a[1]], at[m[0] : m[1]]]) if a else at[m[0] : m[1]]
        for m, a, _ in STREAMS
    ]
    steps = [[(axis, k, ks) for axis, ks in order for k in ks] for _, _, order in STREAMS]
    for n in range(4):
        jobs = [(half_out(v, *st[n]), st[n][0], st[n][1]) for v, st in zip(values, steps)]
        if n < 2:
            jobs.append((half_out(out, "y", RING[n], RING), "y", RING[n]))
        got = start(*jobs)
        values = [
            half_in(v, g, *st[n], (t >> 1) & 3 if st[n][0] == "x" else t >> 3)
            for v, g, st, t in zip(values, got, steps, owners)
        ]
        if n < 2:
            out = half_in(out, got[4], "y", RING[n], RING, owner_out & 3)
    for n in (3, 2, 1, 0):
        jobs = [(v, st[n][0], st[n][1]) for v, st in zip(values, steps)]
        if n == 3:
            jobs.append((out, "z_hi", 1))
        if n < 2:
            jobs.append((out, "y", RING[n]))
        got = start(*jobs)
        values = [join(v, g, *st[n]) for v, g, st in zip(values, got, steps)]
        if n == 3:
            here = (lax.axis_index("z_hi") == (owner_out >> 2)).reshape(2, 1, 1)
            out = jnp.where(here, out, got[4])
        if n < 2:
            out = join(out, got[4], "y", RING[n], RING)
    got = start(*[(v, "core", 1) for v in values])
    full_att = [jnp.concatenate([v[2][:2], v[3][:2]], 0) for v in (values, got)]
    full_mlp = [
        jnp.concatenate([v[2][2:], v[3][2:], v[0], v[1]], 0) for v in (values, got)
    ]

    def whole_of(mine, other):
        return put(jnp.stack([mine, mine]), other[None], 1 - me)

    return whole_of(*full_att).reshape(att.shape), whole_of(*full_mlp).reshape(mlp.shape), out


def reduce_scatter(value, axis):
    n, me = SIZE[axis], lax.axis_index(axis)
    rows = value.shape[0] // n
    got = [swap(block(value, me ^ k, rows).astype(BF), axis, k) for k in range(1, n)]
    return sum([g.astype(F32) for g in got], block(value, me, rows))


def stack(value, axis):
    n, me = SIZE[axis], lax.axis_index(axis)
    out = jnp.stack([value] * n)
    for k in range(1, n):
        out = put(out, swap(value, axis, k)[None], me ^ k)
    return out


TILE = 512


def finish_kernel(tiles_att, me_ref, mine, other, lam_g, basis_out, att, mlp, out_att, out_mlp, whole, lifted):
    step = pl.program_id(0)

    @pl.when(step == 0)
    def _():
        half = mine.shape[3]
        me = me_ref[0]
        for y in range(mine.shape[0]):
            for hi in range(2):
                at = (y * 2 + hi) * 2 * half
                for l in range(2):
                    for c, ref in ((me, mine), (1 - me, other)):
                        rows = pl.ds(pl.multiple_of(at + c * half, half), half)
                        whole[l, rows, :] = ref[y, hi, l].astype(F32)
        for l in range(2):
            core = whole[l, :, :512]
            lam_a = jnp.sum(whole[l, :, 512:], axis=1, keepdims=True)
            gains = lam_g[l : l + 1, :]
            damp = DAMP_REL * jnp.mean(gains) * jnp.mean(lam_a)
            scaled = core / (gains * lam_a + damp)
            high = scaled.astype(BF)
            low = (scaled - high.astype(F32)).astype(BF)
            lifted[l] = (matmul_t(basis_out[l], high) + matmul_t(basis_out[l], low)).astype(BF)

    @pl.when(step < tiles_att)
    def _():
        out_att[...] = matmul_t(lifted[0], att[...]).astype(BF)

    @pl.when(step >= tiles_att)
    def _():
        out_mlp[...] = matmul_t(lifted[1], mlp[...]).astype(BF)


def finish(mine, other, lam_g, basis_out, att, mlp):
    rows = basis_out.shape[1]
    na, nm = att.shape[0] // TILE, mlp.shape[0] // TILE

    def at_att(i):
        return jnp.minimum(i, na - 1)

    def at_mlp(i):
        return jnp.maximum(i - na, 0)

    vmem = pl.BlockSpec(memory_space=pltpu.VMEM)
    return pl.pallas_call(
        functools.partial(finish_kernel, na),
        grid=(na + nm,),
        in_specs=[pl.BlockSpec(memory_space=pltpu.SMEM), vmem, vmem, vmem, vmem]
        + [
            pl.BlockSpec((TILE, 512), lambda i: (at_att(i), 0)),
            pl.BlockSpec((TILE, 512), lambda i: (at_mlp(i), 0)),
        ],
        out_specs=[
            pl.BlockSpec((rows, TILE), lambda i: (0, at_att(i))),
            pl.BlockSpec((rows, TILE), lambda i: (0, at_mlp(i))),
        ],
        out_shape=[
            jax.ShapeDtypeStruct((rows, att.shape[0]), BF),
            jax.ShapeDtypeStruct((rows, mlp.shape[0]), BF),
        ],
        scratch_shapes=[pltpu.VMEM((2, 512, 640), F32), pltpu.VMEM((2, rows, 512), BF)],
        compiler_params=pltpu.CompilerParams(vmem_limit_bytes=24 << 20),
        cost_estimate=pl.CostEstimate(
            flops=2 * rows * 512 * (att.shape[0] + mlp.shape[0]),
            bytes_accessed=8 << 20,
            transcendentals=0,
        ),
        name="finish",
    )(lax.axis_index("core")[None], mine, other, lam_g, basis_out, att, mlp)


def body(
    grad_att,
    grad_mlp,
    acts_att,
    acts_mlp,
    basis_in_att,
    basis_in_mlp,
    basis_out_att,
    basis_out_mlp,
    lam_out,
    owner_dp,
    owner_grad,
):
    rows = grad_att.shape[0]
    tokens_all = rows * 32
    out = jnp.stack(
        [
            jnp.concatenate(
                [v[0], jnp.stack(split3(lam_out[0, l])), jnp.zeros((29, 512), BF)], 0
            )
            for l, v in enumerate((basis_out_att, basis_out_mlp))
        ]
    )
    att, mlp, out = broadcast(basis_in_att[0], basis_in_mlp[0], owner_dp, out, owner_grad)
    basis_out = out[:, :rows]
    lam_g = jnp.sum(out[:, rows : rows + 3].astype(F32), axis=1)

    part = jnp.concatenate(
        [matmul_t(b.T, v) for b, v in ((att, grad_att), (att, acts_att), (mlp, grad_mlp), (mlp, acts_mlp))],
        1,
    )
    part = reduce_scatter(reduce_scatter(part, "y"), "z_hi")

    mine = []
    for l in range(2):
        rot = part[:, 2 * l * rows : (2 * l + 1) * rows]
        proj = part[:, (2 * l + 1) * rows : (2 * l + 2) * rows]
        lam = jnp.sum(proj * proj, axis=1, keepdims=True) / tokens_all
        both = jnp.concatenate([v.astype(BF) for v in split2(rot)], 0)
        both = jnp.dot(both, basis_out[l], preferred_element_type=F32)
        n = rot.shape[0]
        mine.append((both[:n] + both[n:], lam))
    half = part.shape[0] // 2
    me = lax.axis_index("core")
    core = jnp.concatenate([block(c, me, half) for c, _ in mine], 0)
    lam = jnp.concatenate([block(e, me, half) for _, e in mine], 0)
    sent = packed(
        jnp.concatenate([block(c, 1 - me, half) for c, _ in mine], 0),
        jnp.concatenate([block(e, 1 - me, half) for _, e in mine], 0),
    )
    c, e = unpacked(swap(sent, "core"))
    core, lam = core + c, lam + e
    for axis in ("x", "z_lo"):
        sent = packed(core, lam)
        for v in [swap(sent, axis, k) for k in (1, 2, 3)]:
            c, e = unpacked(v)
            core, lam = core + c, lam + e

    wide = packed(core, lam).reshape(2, half, 640)
    wide = stack(stack(wide, "z_hi"), "y")
    (other,) = start((wide, "core", 1))
    return finish(wide, other, lam_g, basis_out, att, mlp)


def solution(mesh):
    fine = Mesh(mesh.devices.reshape(SIZES), AXES)
    placed = (
        P(DP, GRAD),
        P(DP, GRAD),
        P(DP, GRAD),
        P(DP, GRAD),
        P(DP, GRAD, None),
        P(DP, GRAD, None),
        P(GRAD, DP, None),
        P(GRAD, DP, None),
        P(GRAD, None, None),
        P(),
        P(),
    )
    return jax.shard_map(
        body,
        mesh=fine,
        in_specs=placed,
        out_specs=(P(DP, GRAD), P(DP, GRAD)),
        check_vma=False,
    )
```

```python
import functools

import jax
import jax.numpy as jnp
from jax import lax
from jax.experimental import pallas as pl
from jax.experimental.pallas import tpu as pltpu
from jax.sharding import Mesh, PartitionSpec as P

DAMP_REL = 0.1
AXES = ("z_lo", "x", "core", "z_hi", "y")
SIZES = (4, 4, 2, 2, 4)
SIZE = dict(zip(AXES, SIZES))
DP = ("z_lo", "x", "core")
GRAD = ("z_hi", "y")
BF = jnp.bfloat16
F32 = jnp.float32


def block(value, index, rows, axis=0):
    start = [0] * value.ndim
    start[axis] = index * rows
    size = list(value.shape)
    size[axis] = rows
    return lax.dynamic_slice(value, start, size, allow_negative_indices=False)


def put(value, part, index, axis=0):
    start = [0] * value.ndim
    start[axis] = index * part.shape[axis]
    return lax.dynamic_update_slice(value, part, start, allow_negative_indices=False)


def swap(value, axis, k=1):
    return lax.ppermute(value, axis, [(i, i ^ k) for i in range(SIZE[axis])])


def parts_out(value, axis):
    n, me = SIZE[axis], lax.axis_index(axis)
    return [(block(value, me ^ k, value.shape[1] // n, 1), axis, k) for k in range(1, n)]


def part_in(value, got, axis, at):
    n, me = SIZE[axis], lax.axis_index(axis)
    mine = block(value, me, value.shape[1] // n, 1)
    for k, g in enumerate(got, 1):
        mine = jnp.where(((me ^ k) == at).reshape(-1, 1, 1), g, mine)
    return mine


def all_out(value, axis):
    return [(value, axis, k) for k in range(1, SIZE[axis])]


def join(value, got, axis):
    n, me = SIZE[axis], lax.axis_index(axis)
    out = jnp.concatenate([value] * n, 1)
    for k, g in enumerate(got, 1):
        out = put(out, g, me ^ k, 1)
    return out


def start(*jobs):
    held = lax.optimization_barrier(tuple(job[0] for job in jobs))
    return [swap(h, axis, k) for h, (_, axis, k) in zip(held, jobs)]


def split2(value):
    a = lax.reduce_precision(value, 8, 7)
    return a, lax.reduce_precision(value - a, 8, 7)


def split3(value):
    a, b = split2(value)
    return [a.astype(BF), b.astype(BF), (value - a - b).astype(BF)]


def packed(core, lam):
    a, b = split2(lam)
    lane = lax.broadcasted_iota(jnp.int32, (core.shape[0], 128), 1)
    more = jnp.where(lane == 0, a, jnp.where(lane == 1, b, 0.0))
    return jnp.concatenate([core.astype(BF), more.astype(BF)], 1)


def unpacked(value):
    wide = value.astype(F32)
    return wide[:, :512], jnp.sum(wide[:, 512:], axis=1, keepdims=True)


def matmul_t(a, b):
    return lax.dot_general(a, b, (((1,), (1,)), ((), ())), preferred_element_type=F32)


def broadcast(att, mlp, owner, out, owner_out):
    wide = att.shape[1]
    na, nm = att.shape[0] // 256, mlp.shape[0] // 256
    whole = jnp.concatenate([att.reshape(2, na, 128, wide), mlp.reshape(2, nm, 128, wide)], 1)
    cut = (na + nm) // 3
    at = jnp.concatenate([jnp.broadcast_to(owner[0], na), jnp.broadcast_to(owner[1], nm)])
    at_x, at_z = (at >> 1) & 3, at >> 3
    me = lax.axis_index("core")
    got, *got_out = start((block(whole, 1 - me, 1)[0], "core", 1), *parts_out(out, "y"))
    own = (me == (at & 1)).reshape(-1, 1, 1)
    value = jnp.where(own, block(whole, me, 1)[0], got)
    b, a = value[:cut], value[cut:]

    got = start(*parts_out(a, "x"), *parts_out(b, "z_lo"))
    a, b = part_in(a, got[:3], "x", at_x[cut:]), part_in(b, got[3:], "z_lo", at_z[:cut])
    out = part_in(out, got_out, "y", owner_out & 3)
    got = start(*parts_out(a, "z_lo"), *parts_out(b, "x"), (out, "z_hi", 1))
    a, b = part_in(a, got[:3], "z_lo", at_z[cut:]), part_in(b, got[3:6], "x", at_x[:cut])
    here = (lax.axis_index("z_hi") == (owner_out >> 2)).reshape(2, 1, 1)
    out = jnp.where(here, out, got[6])

    got = start(*all_out(a, "z_lo"), *all_out(b, "x"))
    a, b = join(a, got[:3], "z_lo"), join(b, got[3:], "x")
    got = start(*all_out(a, "x"), *all_out(b, "z_lo"))
    a, b = join(a, got[:3], "x"), join(b, got[3:], "z_lo")
    other_b, other_a, *got = start((b, "core", 1), (a, "core", 1), *all_out(out, "y"))

    def whole_of(mine, other):
        return put(jnp.stack([mine, mine]), other[None], 1 - me)

    full_att = whole_of(b[:na], other_b[:na])
    full_mlp = whole_of(
        jnp.concatenate([b[na:], a], 0), jnp.concatenate([other_b[na:], other_a], 0)
    )
    return full_att.reshape(att.shape), full_mlp.reshape(mlp.shape), join(out, got, "y")


def reduce_scatter(value, axis):
    n, me = SIZE[axis], lax.axis_index(axis)
    rows = value.shape[0] // n
    got = [swap(block(value, me ^ k, rows).astype(BF), axis, k) for k in range(1, n)]
    return sum([g.astype(F32) for g in got], block(value, me, rows))


def stack(value, axis):
    n, me = SIZE[axis], lax.axis_index(axis)
    out = jnp.stack([value] * n)
    for k in range(1, n):
        out = put(out, swap(value, axis, k)[None], me ^ k)
    return out


TILE = 512


def finish_kernel(tiles_att, me_ref, mine, other, lam_g, basis_out, att, mlp, out_att, out_mlp, whole, lifted):
    step = pl.program_id(0)

    @pl.when(step == 0)
    def _():
        half = mine.shape[3]
        me = me_ref[0]
        for y in range(mine.shape[0]):
            for hi in range(2):
                at = (y * 2 + hi) * 2 * half
                for l in range(2):
                    for c, ref in ((me, mine), (1 - me, other)):
                        rows = pl.ds(pl.multiple_of(at + c * half, half), half)
                        whole[l, rows, :] = ref[y, hi, l].astype(F32)
        for l in range(2):
            core = whole[l, :, :512]
            lam_a = jnp.sum(whole[l, :, 512:], axis=1, keepdims=True)
            gains = lam_g[l : l + 1, :]
            damp = DAMP_REL * jnp.mean(gains) * jnp.mean(lam_a)
            scaled = core / (gains * lam_a + damp)
            high = scaled.astype(BF)
            low = (scaled - high.astype(F32)).astype(BF)
            lifted[l] = (matmul_t(basis_out[l], high) + matmul_t(basis_out[l], low)).astype(BF)

    @pl.when(step < tiles_att)
    def _():
        out_att[...] = matmul_t(lifted[0], att[...]).astype(BF)

    @pl.when(step >= tiles_att)
    def _():
        out_mlp[...] = matmul_t(lifted[1], mlp[...]).astype(BF)


def finish(mine, other, lam_g, basis_out, att, mlp):
    rows = basis_out.shape[1]
    na, nm = att.shape[0] // TILE, mlp.shape[0] // TILE

    def at_att(i):
        return jnp.minimum(i, na - 1)

    def at_mlp(i):
        return jnp.maximum(i - na, 0)

    vmem = pl.BlockSpec(memory_space=pltpu.VMEM)
    return pl.pallas_call(
        functools.partial(finish_kernel, na),
        grid=(na + nm,),
        in_specs=[pl.BlockSpec(memory_space=pltpu.SMEM), vmem, vmem, vmem, vmem]
        + [
            pl.BlockSpec((TILE, 512), lambda i: (at_att(i), 0)),
            pl.BlockSpec((TILE, 512), lambda i: (at_mlp(i), 0)),
        ],
        out_specs=[
            pl.BlockSpec((rows, TILE), lambda i: (0, at_att(i))),
            pl.BlockSpec((rows, TILE), lambda i: (0, at_mlp(i))),
        ],
        out_shape=[
            jax.ShapeDtypeStruct((rows, att.shape[0]), BF),
            jax.ShapeDtypeStruct((rows, mlp.shape[0]), BF),
        ],
        scratch_shapes=[pltpu.VMEM((2, 512, 640), F32), pltpu.VMEM((2, rows, 512), BF)],
        compiler_params=pltpu.CompilerParams(vmem_limit_bytes=24 << 20),
        cost_estimate=pl.CostEstimate(
            flops=2 * rows * 512 * (att.shape[0] + mlp.shape[0]),
            bytes_accessed=8 << 20,
            transcendentals=0,
        ),
        name="finish",
    )(lax.axis_index("core")[None], mine, other, lam_g, basis_out, att, mlp)


def body(
    grad_att,
    grad_mlp,
    acts_att,
    acts_mlp,
    basis_in_att,
    basis_in_mlp,
    basis_out_att,
    basis_out_mlp,
    lam_out,
    owner_dp,
    owner_grad,
):
    rows = grad_att.shape[0]
    tokens_all = rows * 32
    out = jnp.stack(
        [
            jnp.concatenate(
                [v[0], jnp.stack(split3(lam_out[0, l])), jnp.zeros((29, 512), BF)], 0
            )
            for l, v in enumerate((basis_out_att, basis_out_mlp))
        ]
    )
    att, mlp, out = broadcast(basis_in_att[0], basis_in_mlp[0], owner_dp, out, owner_grad)
    basis_out = out[:, :rows]
    lam_g = jnp.sum(out[:, rows : rows + 3].astype(F32), axis=1)

    part = jnp.concatenate(
        [matmul_t(b.T, v) for b, v in ((att, grad_att), (att, acts_att), (mlp, grad_mlp), (mlp, acts_mlp))],
        1,
    )
    part = reduce_scatter(reduce_scatter(part, "y"), "z_hi")

    mine = []
    for l in range(2):
        rot = part[:, 2 * l * rows : (2 * l + 1) * rows]
        proj = part[:, (2 * l + 1) * rows : (2 * l + 2) * rows]
        lam = jnp.sum(proj * proj, axis=1, keepdims=True) / tokens_all
        both = jnp.concatenate([v.astype(BF) for v in split2(rot)], 0)
        both = jnp.dot(both, basis_out[l], preferred_element_type=F32)
        n = rot.shape[0]
        mine.append((both[:n] + both[n:], lam))
    half = part.shape[0] // 2
    me = lax.axis_index("core")
    core = jnp.concatenate([block(c, me, half) for c, _ in mine], 0)
    lam = jnp.concatenate([block(e, me, half) for _, e in mine], 0)
    sent = packed(
        jnp.concatenate([block(c, 1 - me, half) for c, _ in mine], 0),
        jnp.concatenate([block(e, 1 - me, half) for _, e in mine], 0),
    )
    c, e = unpacked(swap(sent, "core"))
    core, lam = core + c, lam + e
    for axis in ("x", "z_lo"):
        sent = packed(core, lam)
        for v in [swap(sent, axis, k) for k in (1, 2, 3)]:
            c, e = unpacked(v)
            core, lam = core + c, lam + e

    wide = packed(core, lam).reshape(2, half, 640)
    wide = stack(stack(wide, "z_hi"), "y")
    (other,) = start((wide, "core", 1))
    return finish(wide, other, lam_g, basis_out, att, mlp)


def solution(mesh):
    fine = Mesh(mesh.devices.reshape(SIZES), AXES)
    placed = (
        P(DP, GRAD),
        P(DP, GRAD),
        P(DP, GRAD),
        P(DP, GRAD),
        P(DP, GRAD, None),
        P(DP, GRAD, None),
        P(GRAD, DP, None),
        P(GRAD, DP, None),
        P(GRAD, None, None),
        P(),
        P(),
    )
    return jax.shard_map(
        body,
        mesh=fine,
        in_specs=placed,
        out_specs=(P(DP, GRAD), P(DP, GRAD)),
        check_vma=False,
    )
```

```python
import functools

import jax
import jax.numpy as jnp
from jax import lax
from jax.experimental import pallas as pl
from jax.experimental.pallas import tpu as pltpu
from jax.sharding import Mesh, PartitionSpec as P

DAMP_REL = 0.1
AXES = ("z_lo", "x", "core", "z_hi", "y")
SIZES = (4, 4, 2, 2, 4)
SIZE = dict(zip(AXES, SIZES))
DP = ("z_lo", "x", "core")
GRAD = ("z_hi", "y")
BF = jnp.bfloat16
F32 = jnp.float32


def block(value, index, rows, axis=0):
    start = [0] * value.ndim
    start[axis] = index * rows
    size = list(value.shape)
    size[axis] = rows
    return lax.dynamic_slice(value, start, size, allow_negative_indices=False)


def put(value, part, index, axis=0):
    start = [0] * value.ndim
    start[axis] = index * part.shape[axis]
    return lax.dynamic_update_slice(value, part, start, allow_negative_indices=False)


def swap(value, axis, k=1):
    return lax.ppermute(value, axis, [(i, i ^ k) for i in range(SIZE[axis])])


def parts_out(value, axis):
    n, me = SIZE[axis], lax.axis_index(axis)
    return [(block(value, me ^ k, value.shape[1] // n, 1), axis, k) for k in range(1, n)]


def part_in(value, got, axis, at):
    n, me = SIZE[axis], lax.axis_index(axis)
    mine = block(value, me, value.shape[1] // n, 1)
    for k, g in enumerate(got, 1):
        mine = jnp.where(((me ^ k) == at).reshape(-1, 1, 1), g, mine)
    return mine


def all_out(value, axis):
    return [(value, axis, k) for k in range(1, SIZE[axis])]


def join(value, got, axis):
    n, me = SIZE[axis], lax.axis_index(axis)
    out = jnp.concatenate([value] * n, 1)
    for k, g in enumerate(got, 1):
        out = put(out, g, me ^ k, 1)
    return out


def start(*jobs):
    held = lax.optimization_barrier(tuple(job[0] for job in jobs))
    return [swap(h, axis, k) for h, (_, axis, k) in zip(held, jobs)]


def split2(value):
    a = lax.reduce_precision(value, 8, 7)
    return a, lax.reduce_precision(value - a, 8, 7)


def split3(value):
    a, b = split2(value)
    return [a.astype(BF), b.astype(BF), (value - a - b).astype(BF)]


def packed(core, lam):
    a, b = split2(lam)
    lane = lax.broadcasted_iota(jnp.int32, (core.shape[0], 128), 1)
    more = jnp.where(lane == 0, a, jnp.where(lane == 1, b, 0.0))
    return jnp.concatenate([core.astype(BF), more.astype(BF)], 1)


def unpacked(value):
    wide = value.astype(F32)
    return wide[:, :512], jnp.sum(wide[:, 512:], axis=1, keepdims=True)


def matmul_t(a, b):
    return lax.dot_general(a, b, (((1,), (1,)), ((), ())), preferred_element_type=F32)


def broadcast(att, mlp, owner, out, owner_out):
    wide = att.shape[1]
    na, nm = att.shape[0] // 256, mlp.shape[0] // 256
    whole = jnp.concatenate([att.reshape(2, na, 128, wide), mlp.reshape(2, nm, 128, wide)], 1)
    cut = (na + nm) // 3
    at = jnp.concatenate([jnp.broadcast_to(owner[0], na), jnp.broadcast_to(owner[1], nm)])
    at_x, at_z = (at >> 1) & 3, at >> 3
    me = lax.axis_index("core")
    (got,) = start((block(whole, 1 - me, 1)[0], "core", 1))
    got_out = start(*parts_out(out, "y"))
    own = (me == (at & 1)).reshape(-1, 1, 1)
    value = jnp.where(own, block(whole, me, 1)[0], got)
    b, a = value[:cut], value[cut:]

    got = start(*parts_out(a, "x"), *parts_out(b, "z_lo"))
    a, b = part_in(a, got[:3], "x", at_x[cut:]), part_in(b, got[3:], "z_lo", at_z[:cut])
    out = part_in(out, got_out, "y", owner_out & 3)
    got = start(*parts_out(a, "z_lo"), *parts_out(b, "x"), (out, "z_hi", 1))
    a, b = part_in(a, got[:3], "z_lo", at_z[cut:]), part_in(b, got[3:6], "x", at_x[:cut])
    here = (lax.axis_index("z_hi") == (owner_out >> 2)).reshape(2, 1, 1)
    out = jnp.where(here, out, got[6])

    got = start(*all_out(a, "z_lo"), *all_out(b, "x"))
    a, b = join(a, got[:3], "z_lo"), join(b, got[3:], "x")
    got = start(*all_out(a, "x"), *all_out(b, "z_lo"))
    a, b = join(a, got[:3], "x"), join(b, got[3:], "z_lo")
    other_b, other_a, *got = start((b, "core", 1), (a, "core", 1), *all_out(out, "y"))

    def whole_of(mine, other):
        return put(jnp.stack([mine, mine]), other[None], 1 - me)

    full_att = whole_of(b[:na], other_b[:na])
    full_mlp = whole_of(
        jnp.concatenate([b[na:], a], 0), jnp.concatenate([other_b[na:], other_a], 0)
    )
    halves = ((b, a), (other_b, other_a))
    return full_att.reshape(att.shape), full_mlp.reshape(mlp.shape), halves, join(out, got, "y")


def reduce_scatter(value, sent, axis):
    n, me = SIZE[axis], lax.axis_index(axis)
    rows = value.shape[0] // n
    got = [swap(block(sent, me ^ k, rows), axis, k) for k in range(1, n)]
    return sum([g.astype(F32) for g in got], block(value, me, rows))


def stack(value, axis):
    n, me = SIZE[axis], lax.axis_index(axis)
    out = jnp.stack([value] * n)
    for k in range(1, n):
        out = put(out, swap(value, axis, k)[None], me ^ k)
    return out


def windows_kernel(n_att, core_ref, b, a, *refs):
    grads, (acc, out), turned = refs[:4], refs[4:6], refs[6:]
    for i, g in enumerate(grads):
        rows = pl.ds(i * g.shape[0], g.shape[0])
        if i < 2:
            total = jnp.dot(g[...], b[:n_att, :], preferred_element_type=F32)
        else:
            n = b.shape[0] - n_att
            total = jnp.dot(g[:, :n], b[n_att:, :], preferred_element_type=F32)
            total += jnp.dot(g[:, n:], a[...], preferred_element_type=F32)
        total += acc[rows, :]
        if turned:
            total = total.T
            out[:, rows] = total
            turned[0][:, rows] = total.astype(BF)
        else:
            out[rows, :] = total


def windows(core, half, blocks, acc, last):
    b, a = (v.reshape(-1, v.shape[-1]) for v in half)
    n_att = blocks[0].shape[1] // 2
    rows = 4 * blocks[0].shape[0]
    vmem = pl.BlockSpec(memory_space=pltpu.VMEM)
    shape = (512, rows) if last else (rows, 512)
    return pl.pallas_call(
        functools.partial(windows_kernel, n_att),
        grid_spec=pltpu.PrefetchScalarGridSpec(
            num_scalar_prefetch=1,
            grid=(1,),
            in_specs=[vmem, vmem]
            + [
                pl.BlockSpec((v.shape[0], v.shape[1] // 2), lambda i, c: (0, c[0]))
                for v in blocks
            ]
            + [vmem],
            out_specs=[vmem] * (1 + last),
        ),
        out_shape=[jax.ShapeDtypeStruct(shape, F32), jax.ShapeDtypeStruct(shape, BF)][: 1 + last],
        compiler_params=pltpu.CompilerParams(vmem_limit_bytes=24 << 20),
        cost_estimate=pl.CostEstimate(
            flops=rows * 512 * (b.shape[0] + a.shape[0]),
            bytes_accessed=8 << 20,
            transcendentals=0,
        ),
        name="windows",
    )(core[None], b, a, *blocks, acc)


TILE = 512


def finish_kernel(tiles_att, me_ref, mine, other, lam_g, basis_out, att, mlp, out_att, out_mlp, whole, lifted):
    step = pl.program_id(0)

    @pl.when(step == 0)
    def _():
        half = mine.shape[3]
        me = me_ref[0]
        for y in range(mine.shape[0]):
            for hi in range(2):
                at = (y * 2 + hi) * 2 * half
                for l in range(2):
                    for c, ref in ((me, mine), (1 - me, other)):
                        rows = pl.ds(pl.multiple_of(at + c * half, half), half)
                        whole[l, rows, :] = ref[y, hi, l].astype(F32)
        for l in range(2):
            core = whole[l, :, :512]
            lam_a = jnp.sum(whole[l, :, 512:], axis=1, keepdims=True)
            gains = lam_g[l : l + 1, :]
            damp = DAMP_REL * jnp.mean(gains) * jnp.mean(lam_a)
            scaled = core / (gains * lam_a + damp)
            high = scaled.astype(BF)
            low = (scaled - high.astype(F32)).astype(BF)
            lifted[l] = (matmul_t(basis_out[l], high) + matmul_t(basis_out[l], low)).astype(BF)

    @pl.when(step < tiles_att)
    def _():
        out_att[...] = matmul_t(lifted[0], att[...]).astype(BF)

    @pl.when(step >= tiles_att)
    def _():
        out_mlp[...] = matmul_t(lifted[1], mlp[...]).astype(BF)


def finish(mine, other, lam_g, basis_out, att, mlp):
    rows = basis_out.shape[1]
    na, nm = att.shape[0] // TILE, mlp.shape[0] // TILE

    def at_att(i):
        return jnp.minimum(i, na - 1)

    def at_mlp(i):
        return jnp.maximum(i - na, 0)

    vmem = pl.BlockSpec(memory_space=pltpu.VMEM)
    return pl.pallas_call(
        functools.partial(finish_kernel, na),
        grid=(na + nm,),
        in_specs=[pl.BlockSpec(memory_space=pltpu.SMEM), vmem, vmem, vmem, vmem]
        + [
            pl.BlockSpec((TILE, 512), lambda i: (at_att(i), 0)),
            pl.BlockSpec((TILE, 512), lambda i: (at_mlp(i), 0)),
        ],
        out_specs=[
            pl.BlockSpec((rows, TILE), lambda i: (0, at_att(i))),
            pl.BlockSpec((rows, TILE), lambda i: (0, at_mlp(i))),
        ],
        out_shape=[
            jax.ShapeDtypeStruct((rows, att.shape[0]), BF),
            jax.ShapeDtypeStruct((rows, mlp.shape[0]), BF),
        ],
        scratch_shapes=[pltpu.VMEM((2, 512, 640), F32), pltpu.VMEM((2, rows, 512), BF)],
        compiler_params=pltpu.CompilerParams(vmem_limit_bytes=24 << 20),
        cost_estimate=pl.CostEstimate(
            flops=2 * rows * 512 * (att.shape[0] + mlp.shape[0]),
            bytes_accessed=8 << 20,
            transcendentals=0,
        ),
        name="finish",
    )(lax.axis_index("core")[None], mine, other, lam_g, basis_out, att, mlp)


def body(
    grad_att,
    grad_mlp,
    acts_att,
    acts_mlp,
    basis_in_att,
    basis_in_mlp,
    basis_out_att,
    basis_out_mlp,
    lam_out,
    owner_dp,
    owner_grad,
):
    rows = grad_att.shape[0]
    tokens_all = rows * 32
    out = jnp.stack(
        [
            jnp.concatenate(
                [v[0], jnp.stack(split3(lam_out[0, l])), jnp.zeros((29, 512), BF)], 0
            )
            for l, v in enumerate((basis_out_att, basis_out_mlp))
        ]
    )
    att, mlp, halves, out = broadcast(basis_in_att[0], basis_in_mlp[0], owner_dp, out, owner_grad)
    basis_out = out[:, :rows]
    lam_g = jnp.sum(out[:, rows : rows + 3].astype(F32), axis=1)

    me = lax.axis_index("core")
    blocks = (grad_att, acts_att, grad_mlp, acts_mlp)
    (acc,) = windows(me, halves[0], blocks, jnp.zeros((4 * rows, 512), F32), False)
    part, sent = windows(1 - me, halves[1], blocks, acc, True)
    part = reduce_scatter(part, sent, "y")
    part = reduce_scatter(part, part.astype(BF), "z_hi")

    mine = []
    for l in range(2):
        rot = part[:, 2 * l * rows : (2 * l + 1) * rows]
        proj = part[:, (2 * l + 1) * rows : (2 * l + 2) * rows]
        lam = jnp.sum(proj * proj, axis=1, keepdims=True) / tokens_all
        both = jnp.concatenate([v.astype(BF) for v in split2(rot)], 0)
        both = jnp.dot(both, basis_out[l], preferred_element_type=F32)
        n = rot.shape[0]
        mine.append((both[:n] + both[n:], lam))
    half = part.shape[0] // 2
    me = lax.axis_index("core")
    core = jnp.concatenate([block(c, me, half) for c, _ in mine], 0)
    lam = jnp.concatenate([block(e, me, half) for _, e in mine], 0)
    sent = packed(
        jnp.concatenate([block(c, 1 - me, half) for c, _ in mine], 0),
        jnp.concatenate([block(e, 1 - me, half) for _, e in mine], 0),
    )
    c, e = unpacked(swap(sent, "core"))
    core, lam = core + c, lam + e
    for axis in ("x", "z_lo"):
        sent = packed(core, lam)
        for v in [swap(sent, axis, k) for k in (1, 2, 3)]:
            c, e = unpacked(v)
            core, lam = core + c, lam + e

    wide = packed(core, lam).reshape(2, half, 640)
    wide = stack(stack(wide, "z_hi"), "y")
    (other,) = start((wide, "core", 1))
    return finish(wide, other, lam_g, basis_out, att, mlp)


def solution(mesh):
    fine = Mesh(mesh.devices.reshape(SIZES), AXES)
    placed = (
        P(DP, GRAD),
        P(DP, GRAD),
        P(DP, GRAD),
        P(DP, GRAD),
        P(DP, GRAD, None),
        P(DP, GRAD, None),
        P(GRAD, DP, None),
        P(GRAD, DP, None),
        P(GRAD, None, None),
        P(),
        P(),
    )
    return jax.shard_map(
        body,
        mesh=fine,
        in_specs=placed,
        out_specs=(P(DP, GRAD), P(DP, GRAD)),
        check_vma=False,
    )
```

```python
import functools

import jax
import jax.numpy as jnp
from jax import lax
from jax.experimental import pallas as pl
from jax.experimental.pallas import tpu as pltpu
from jax.sharding import Mesh, PartitionSpec as P

DAMP_REL = 0.1
AXES = ("z_lo", "x", "core", "z_hi", "y")
SIZES = (4, 4, 2, 2, 4)
SIZE = dict(zip(AXES, SIZES))
DP = ("z_lo", "x", "core")
GRAD = ("z_hi", "y")
BF = jnp.bfloat16
F32 = jnp.float32


def block(value, index, rows, axis=0):
    start = [0] * value.ndim
    start[axis] = index * rows
    size = list(value.shape)
    size[axis] = rows
    return lax.dynamic_slice(value, start, size, allow_negative_indices=False)


def put(value, part, index, axis=0):
    start = [0] * value.ndim
    start[axis] = index * part.shape[axis]
    return lax.dynamic_update_slice(value, part, start, allow_negative_indices=False)


def swap(value, axis, k=1):
    return lax.ppermute(value, axis, [(i, i ^ k) for i in range(SIZE[axis])])


def parts_out(value, axis):
    n, me = SIZE[axis], lax.axis_index(axis)
    return [(block(value, me ^ k, value.shape[1] // n, 1), axis, k) for k in range(1, n)]


def part_in(value, got, axis, at):
    n, me = SIZE[axis], lax.axis_index(axis)
    mine = block(value, me, value.shape[1] // n, 1)
    for k, g in enumerate(got, 1):
        mine = jnp.where(((me ^ k) == at).reshape(-1, 1, 1), g, mine)
    return mine


def all_out(value, axis):
    return [(value, axis, k) for k in range(1, SIZE[axis])]


def join(value, got, axis):
    n, me = SIZE[axis], lax.axis_index(axis)
    out = jnp.concatenate([value] * n, 1)
    for k, g in enumerate(got, 1):
        out = put(out, g, me ^ k, 1)
    return out


def start(*jobs, after=()):
    held = lax.optimization_barrier(tuple(job[0] for job in jobs) + tuple(after))
    return [swap(h, axis, k) for h, (_, axis, k) in zip(held, jobs)]


def split2(value):
    a = lax.reduce_precision(value, 8, 7)
    return a, lax.reduce_precision(value - a, 8, 7)


def split3(value):
    a, b = split2(value)
    return [a.astype(BF), b.astype(BF), (value - a - b).astype(BF)]


def packed(core, lam):
    a, b = split2(lam)
    lane = lax.broadcasted_iota(jnp.int32, (core.shape[0], 128), 1)
    more = jnp.where(lane == 0, a, jnp.where(lane == 1, b, 0.0))
    return jnp.concatenate([core.astype(BF), more.astype(BF)], 1)


def unpacked(value):
    wide = value.astype(F32)
    return wide[:, :512], jnp.sum(wide[:, 512:], axis=1, keepdims=True)


def matmul_t(a, b):
    return lax.dot_general(a, b, (((1,), (1,)), ((), ())), preferred_element_type=F32)


def broadcast(att, mlp, owner, out, owner_out):
    wide = att.shape[1]
    na, nm = att.shape[0] // 256, mlp.shape[0] // 256
    whole = jnp.concatenate([att.reshape(2, na, 128, wide), mlp.reshape(2, nm, 128, wide)], 1)
    cut = (na + nm) // 3
    at = jnp.concatenate([jnp.broadcast_to(owner[0], na), jnp.broadcast_to(owner[1], nm)])
    at_x, at_z = (at >> 1) & 3, at >> 3
    me = lax.axis_index("core")
    (got,) = start((block(whole, 1 - me, 1)[0], "core", 1))
    got_out = start(*parts_out(out, "y"))
    own = (me == (at & 1)).reshape(-1, 1, 1)
    value = jnp.where(own, block(whole, me, 1)[0], got)
    b, a = value[:cut], value[cut:]

    got = start(*parts_out(a, "x"), *parts_out(b, "z_lo"))
    a, b = part_in(a, got[:3], "x", at_x[cut:]), part_in(b, got[3:], "z_lo", at_z[:cut])
    out = part_in(out, got_out, "y", owner_out & 3)
    got = start(*parts_out(a, "z_lo"), *parts_out(b, "x"), (out, "z_hi", 1))
    a, b = part_in(a, got[:3], "z_lo", at_z[cut:]), part_in(b, got[3:6], "x", at_x[:cut])
    here = (lax.axis_index("z_hi") == (owner_out >> 2)).reshape(2, 1, 1)
    out = jnp.where(here, out, got[6])
    out_there = got[6:]

    got = start(*all_out(a, "z_lo"), *all_out(b, "x"))
    a, b = join(a, got[:3], "z_lo"), join(b, got[3:], "x")
    got = start(*all_out(a, "x"), *all_out(b, "z_lo"), after=out_there)
    got_out = start(*all_out(out, "y"), after=got[3:4])
    a, b = join(a, got[:3], "x"), join(b, got[3:], "z_lo")
    other_b, other_a = start((b, "core", 1), (a, "core", 1), after=got_out)

    def whole_of(mine, other):
        return put(jnp.stack([mine, mine]), other[None], 1 - me)

    full_att = whole_of(b[:na], other_b[:na])
    full_mlp = whole_of(
        jnp.concatenate([b[na:], a], 0), jnp.concatenate([other_b[na:], other_a], 0)
    )
    halves = ((b, a), (other_b, other_a))
    return full_att.reshape(att.shape), full_mlp.reshape(mlp.shape), halves, join(out, got_out, "y")


def add_up(mine, sent, axis):
    got = [swap(v, axis, k) for k, v in enumerate(sent, 1)]
    return sum([g.astype(F32) for g in got], mine)


def stack(value, axis):
    n, me = SIZE[axis], lax.axis_index(axis)
    out = jnp.stack([value] * n)
    for k in range(1, n):
        out = put(out, swap(value, axis, k)[None], me ^ k)
    return out


def windows_kernel(n_att, last, at_ref, b, a, *refs):
    whole, acc = refs[:4], refs[4]
    outs = refs[5 : 9 if last else 6]
    turned, held, sems = refs[9 if last else 6] if last else None, refs[-5:-1], refs[-1]
    copies = []
    for i in range(4):
        n = held[i].shape[1]
        columns = pl.ds(pl.multiple_of(at_ref[0] * n, n), n)
        copies.append(pltpu.make_async_copy(whole[i].at[:, columns], held[i], sems.at[i]))
        copies[i].start()
    for i in range(4):
        g = held[i]
        rows = pl.ds(i * g.shape[0], g.shape[0])
        copies[i].wait()
        if i < 2:
            total = jnp.dot(g[...], b[:n_att, :], preferred_element_type=F32)
        else:
            n = b.shape[0] - n_att
            total = jnp.dot(g[:, :n], b[n_att:, :], preferred_element_type=F32)
            total += jnp.dot(g[:, n:], a[...], preferred_element_type=F32)
        total += acc[rows, :]
        if last:
            turned[:, rows] = total.T
        else:
            outs[0][rows, :] = total
    if last:
        n = outs[0].shape[0]
        for k, out in enumerate(outs):
            piece = at_ref[1] ^ k
            out[...] = turned[pl.ds(pl.multiple_of(piece * n, n), n), :].astype(out.dtype)


def windows(core, half, blocks, acc, last):
    b, a = (v.reshape(-1, v.shape[-1]) for v in half)
    n_att = blocks[0].shape[1] // 2
    rows = 4 * blocks[0].shape[0]
    vmem = pl.BlockSpec(memory_space=pltpu.VMEM)
    if last:
        shapes = [jax.ShapeDtypeStruct((128, rows), t) for t in (F32, BF, BF, BF)]
    else:
        shapes = [jax.ShapeDtypeStruct((rows, 512), F32)]
    return pl.pallas_call(
        functools.partial(windows_kernel, n_att, last),
        in_specs=[pl.BlockSpec(memory_space=pltpu.SMEM), vmem, vmem]
        + [pl.BlockSpec(memory_space=pltpu.HBM)] * 4
        + [vmem],
        out_specs=[vmem] * len(shapes),
        out_shape=shapes,
        scratch_shapes=[pltpu.VMEM((512, rows), F32)] * last
        + [pltpu.VMEM((v.shape[0], v.shape[1] // 2), BF) for v in blocks]
        + [pltpu.SemaphoreType.DMA((4,))],
        compiler_params=pltpu.CompilerParams(vmem_limit_bytes=24 << 20),
        cost_estimate=pl.CostEstimate(
            flops=rows * 512 * (b.shape[0] + a.shape[0]),
            bytes_accessed=8 << 20,
            transcendentals=0,
        ),
        name="windows",
    )(jnp.stack([core, lax.axis_index("y")]), b, a, *blocks, acc)


TILE = 512


def finish_kernel(tiles_att, me_ref, mine, other, lam_g, basis_out, att, mlp, out_att, out_mlp, whole, lifted):
    step = pl.program_id(0)

    @pl.when(step == 0)
    def _():
        half = mine.shape[3]
        me = me_ref[0]
        for y in range(mine.shape[0]):
            for hi in range(2):
                at = (y * 2 + hi) * 2 * half
                for l in range(2):
                    for c, ref in ((me, mine), (1 - me, other)):
                        rows = pl.ds(pl.multiple_of(at + c * half, half), half)
                        whole[l, rows, :] = ref[y, hi, l].astype(F32)
        for l in range(2):
            core = whole[l, :, :512]
            lam_a = jnp.sum(whole[l, :, 512:], axis=1, keepdims=True)
            gains = lam_g[l : l + 1, :]
            damp = DAMP_REL * jnp.mean(gains) * jnp.mean(lam_a)
            scaled = core / (gains * lam_a + damp)
            high = scaled.astype(BF)
            low = (scaled - high.astype(F32)).astype(BF)
            lifted[l] = (matmul_t(basis_out[l], high) + matmul_t(basis_out[l], low)).astype(BF)

    @pl.when(step < tiles_att)
    def _():
        out_att[...] = matmul_t(lifted[0], att[...]).astype(BF)

    @pl.when(step >= tiles_att)
    def _():
        out_mlp[...] = matmul_t(lifted[1], mlp[...]).astype(BF)


def finish(mine, other, lam_g, basis_out, att, mlp):
    rows = basis_out.shape[1]
    na, nm = att.shape[0] // TILE, mlp.shape[0] // TILE

    def at_att(i):
        return jnp.minimum(i, na - 1)

    def at_mlp(i):
        return jnp.maximum(i - na, 0)

    vmem = pl.BlockSpec(memory_space=pltpu.VMEM)
    return pl.pallas_call(
        functools.partial(finish_kernel, na),
        grid=(na + nm,),
        in_specs=[pl.BlockSpec(memory_space=pltpu.SMEM), vmem, vmem, vmem, vmem]
        + [
            pl.BlockSpec((TILE, 512), lambda i: (at_att(i), 0)),
            pl.BlockSpec((TILE, 512), lambda i: (at_mlp(i), 0)),
        ],
        out_specs=[
            pl.BlockSpec((rows, TILE), lambda i: (0, at_att(i))),
            pl.BlockSpec((rows, TILE), lambda i: (0, at_mlp(i))),
        ],
        out_shape=[
            jax.ShapeDtypeStruct((rows, att.shape[0]), BF),
            jax.ShapeDtypeStruct((rows, mlp.shape[0]), BF),
        ],
        scratch_shapes=[pltpu.VMEM((2, 512, 640), F32), pltpu.VMEM((2, rows, 512), BF)],
        compiler_params=pltpu.CompilerParams(vmem_limit_bytes=24 << 20),
        cost_estimate=pl.CostEstimate(
            flops=2 * rows * 512 * (att.shape[0] + mlp.shape[0]),
            bytes_accessed=8 << 20,
            transcendentals=0,
        ),
        name="finish",
    )(lax.axis_index("core")[None], mine, other, lam_g, basis_out, att, mlp)


def body(
    grad_att,
    grad_mlp,
    acts_att,
    acts_mlp,
    basis_in_att,
    basis_in_mlp,
    basis_out_att,
    basis_out_mlp,
    lam_out,
    owner_dp,
    owner_grad,
):
    rows = grad_att.shape[0]
    tokens_all = rows * 32
    out = jnp.stack(
        [
            jnp.concatenate(
                [v[0], jnp.stack(split3(lam_out[0, l])), jnp.zeros((29, 512), BF)], 0
            )
            for l, v in enumerate((basis_out_att, basis_out_mlp))
        ]
    )
    att, mlp, halves, out = broadcast(basis_in_att[0], basis_in_mlp[0], owner_dp, out, owner_grad)
    basis_out = out[:, :rows]
    lam_g = jnp.sum(out[:, rows : rows + 3].astype(F32), axis=1)

    me = lax.axis_index("core")
    blocks = (grad_att, acts_att, grad_mlp, acts_mlp)
    (acc,) = windows(me, halves[0], blocks, jnp.zeros((4 * rows, 512), F32), False)
    part, *sent = windows(1 - me, halves[1], blocks, acc, True)
    part = add_up(part, sent, "y")
    hi, half = lax.axis_index("z_hi"), part.shape[0] // 2
    part = add_up(block(part, hi, half), [block(part, 1 - hi, half).astype(BF)], "z_hi")

    mine = []
    for l in range(2):
        rot = part[:, 2 * l * rows : (2 * l + 1) * rows]
        proj = part[:, (2 * l + 1) * rows : (2 * l + 2) * rows]
        lam = jnp.sum(proj * proj, axis=1, keepdims=True) / tokens_all
        both = jnp.concatenate([v.astype(BF) for v in split2(rot)], 0)
        both = jnp.dot(both, basis_out[l], preferred_element_type=F32)
        n = rot.shape[0]
        mine.append((both[:n] + both[n:], lam))
    half = part.shape[0] // 2
    me = lax.axis_index("core")
    core = jnp.concatenate([block(c, me, half) for c, _ in mine], 0)
    lam = jnp.concatenate([block(e, me, half) for _, e in mine], 0)
    sent = packed(
        jnp.concatenate([block(c, 1 - me, half) for c, _ in mine], 0),
        jnp.concatenate([block(e, 1 - me, half) for _, e in mine], 0),
    )
    c, e = unpacked(swap(sent, "core"))
    core, lam = core + c, lam + e
    for axis in ("x", "z_lo"):
        sent = packed(core, lam)
        for v in [swap(sent, axis, k) for k in (1, 2, 3)]:
            c, e = unpacked(v)
            core, lam = core + c, lam + e

    wide = packed(core, lam).reshape(2, half, 640)
    wide = stack(stack(wide, "z_hi"), "y")
    (other,) = start((wide, "core", 1))
    return finish(wide, other, lam_g, basis_out, att, mlp)


def solution(mesh):
    fine = Mesh(mesh.devices.reshape(SIZES), AXES)
    placed = (
        P(DP, GRAD),
        P(DP, GRAD),
        P(DP, GRAD),
        P(DP, GRAD),
        P(DP, GRAD, None),
        P(DP, GRAD, None),
        P(GRAD, DP, None),
        P(GRAD, DP, None),
        P(GRAD, None, None),
        P(),
        P(),
    )
    return jax.shard_map(
        body,
        mesh=fine,
        in_specs=placed,
        out_specs=(P(DP, GRAD), P(DP, GRAD)),
        check_vma=False,
    )
```

```python
import functools

import jax
import jax.numpy as jnp
from jax import lax
from jax.experimental import pallas as pl
from jax.experimental.pallas import tpu as pltpu
from jax.sharding import Mesh, PartitionSpec as P

DAMP_REL = 0.1
AXES = ("z_lo", "x", "core", "z_hi", "y")
SIZES = (4, 4, 2, 2, 4)
SIZE = dict(zip(AXES, SIZES))
DP = ("z_lo", "x", "core")
GRAD = ("z_hi", "y")
BF = jnp.bfloat16
F32 = jnp.float32


def block(value, index, rows, axis=0):
    start = [0] * value.ndim
    start[axis] = index * rows
    size = list(value.shape)
    size[axis] = rows
    return lax.dynamic_slice(value, start, size, allow_negative_indices=False)


def put(value, part, index, axis=0):
    start = [0] * value.ndim
    start[axis] = index * part.shape[axis]
    return lax.dynamic_update_slice(value, part, start, allow_negative_indices=False)


def swap(value, axis, k=1):
    return lax.ppermute(value, axis, [(i, i ^ k) for i in range(SIZE[axis])])


def parts_out(value, axis):
    n, me = SIZE[axis], lax.axis_index(axis)
    return [(block(value, me ^ k, value.shape[1] // n, 1), axis, k) for k in range(1, n)]


def part_in(value, got, axis, at):
    n, me = SIZE[axis], lax.axis_index(axis)
    mine = block(value, me, value.shape[1] // n, 1)
    for k, g in enumerate(got, 1):
        mine = jnp.where(((me ^ k) == at).reshape(-1, 1, 1), g, mine)
    return mine


def all_out(value, axis):
    return [(value, axis, k) for k in range(1, SIZE[axis])]


def join(value, got, axis):
    n, me = SIZE[axis], lax.axis_index(axis)
    out = jnp.concatenate([value] * n, 1)
    for k, g in enumerate(got, 1):
        out = put(out, g, me ^ k, 1)
    return out


def start(*jobs, after=()):
    held = lax.optimization_barrier(tuple(job[0] for job in jobs) + tuple(after))
    return [swap(h, axis, k) for h, (_, axis, k) in zip(held, jobs)]


def split2(value):
    a = lax.reduce_precision(value, 8, 7)
    return a, lax.reduce_precision(value - a, 8, 7)


def split3(value):
    a, b = split2(value)
    return [a.astype(BF), b.astype(BF), (value - a - b).astype(BF)]


def packed(core, lam):
    a, b = split2(lam)
    lane = lax.broadcasted_iota(jnp.int32, (core.shape[0], 128), 1)
    more = jnp.where(lane == 0, a, jnp.where(lane == 1, b, 0.0))
    return jnp.concatenate([core.astype(BF), more.astype(BF)], 1)


def unpacked(value):
    wide = value.astype(F32)
    return wide[:, :512], jnp.sum(wide[:, 512:], axis=1, keepdims=True)


def matmul_t(a, b):
    return lax.dot_general(a, b, (((1,), (1,)), ((), ())), preferred_element_type=F32)


def broadcast(att, mlp, owner, out, owner_out):
    wide = att.shape[1]
    na, nm = att.shape[0] // 256, mlp.shape[0] // 256
    whole = jnp.concatenate([att.reshape(2, na, 128, wide), mlp.reshape(2, nm, 128, wide)], 1)
    cut = (na + nm) // 3
    at = jnp.concatenate([jnp.broadcast_to(owner[0], na), jnp.broadcast_to(owner[1], nm)])
    at_x, at_z = (at >> 1) & 3, at >> 3
    me = lax.axis_index("core")
    (got,) = start((block(whole, 1 - me, 1)[0], "core", 1))
    got_out = start(*parts_out(out, "y"))
    own = (me == (at & 1)).reshape(-1, 1, 1)
    value = jnp.where(own, block(whole, me, 1)[0], got)
    b, a = value[:cut], value[cut:]

    got = start(*parts_out(a, "x"), *parts_out(b, "z_lo"))
    a, b = part_in(a, got[:3], "x", at_x[cut:]), part_in(b, got[3:], "z_lo", at_z[:cut])
    out = part_in(out, got_out, "y", owner_out & 3)
    got = start(*parts_out(a, "z_lo"), *parts_out(b, "x"), (out, "z_hi", 1))
    a, b = part_in(a, got[:3], "z_lo", at_z[cut:]), part_in(b, got[3:6], "x", at_x[:cut])
    here = (lax.axis_index("z_hi") == (owner_out >> 2)).reshape(2, 1, 1)
    out = jnp.where(here, out, got[6])

    got = start(*all_out(a, "z_lo"), *all_out(b, "x"), *all_out(out, "y"))
    a, b = join(a, got[:3], "z_lo"), join(b, got[3:6], "x")
    got_out = got[6:]
    got = start(*all_out(a, "x"), *all_out(b, "z_lo"), after=got_out)
    a, b = join(a, got[:3], "x"), join(b, got[3:], "z_lo")
    other_b, other_a = start((b, "core", 1), (a, "core", 1))

    def whole_of(mine, other):
        return put(jnp.stack([mine, mine]), other[None], 1 - me)

    full_att = whole_of(b[:na], other_b[:na])
    full_mlp = whole_of(
        jnp.concatenate([b[na:], a], 0), jnp.concatenate([other_b[na:], other_a], 0)
    )
    halves = ((b, a), (other_b, other_a))
    return full_att.reshape(att.shape), full_mlp.reshape(mlp.shape), halves, join(out, got_out, "y")


def add_up(mine, sent, axis):
    got = [swap(v, axis, k) for k, v in enumerate(sent, 1)]
    return sum([g.astype(F32) for g in got], mine)


def stack(value, axis):
    n, me = SIZE[axis], lax.axis_index(axis)
    out = jnp.stack([value] * n)
    for k in range(1, n):
        out = put(out, swap(value, axis, k)[None], me ^ k)
    return out


def windows_kernel(n_att, last, at_ref, b, a, *refs):
    whole, acc = refs[:4], refs[4]
    outs = refs[5 : 9 if last else 6]
    turned, held, sems = refs[9 if last else 6] if last else None, refs[-5:-1], refs[-1]
    copies = []
    for i in range(4):
        n = held[i].shape[1]
        columns = pl.ds(pl.multiple_of(at_ref[0] * n, n), n)
        copies.append(pltpu.make_async_copy(whole[i].at[:, columns], held[i], sems.at[i]))
        copies[i].start()
    for i in range(4):
        g = held[i]
        rows = pl.ds(i * g.shape[0], g.shape[0])
        copies[i].wait()
        if i < 2:
            total = jnp.dot(g[...], b[:n_att, :], preferred_element_type=F32)
        else:
            n = b.shape[0] - n_att
            total = jnp.dot(g[:, :n], b[n_att:, :], preferred_element_type=F32)
            total += jnp.dot(g[:, n:], a[...], preferred_element_type=F32)
        total += acc[rows, :]
        if last:
            turned[:, rows] = total.T
        else:
            outs[0][rows, :] = total
    if last:
        n = outs[0].shape[0]
        for k, out in enumerate(outs):
            piece = at_ref[1] ^ k
            out[...] = turned[pl.ds(pl.multiple_of(piece * n, n), n), :].astype(out.dtype)


def windows(core, half, blocks, acc, last):
    b, a = (v.reshape(-1, v.shape[-1]) for v in half)
    n_att = blocks[0].shape[1] // 2
    rows = 4 * blocks[0].shape[0]
    vmem = pl.BlockSpec(memory_space=pltpu.VMEM)
    if last:
        shapes = [jax.ShapeDtypeStruct((128, rows), t) for t in (F32, BF, BF, BF)]
    else:
        shapes = [jax.ShapeDtypeStruct((rows, 512), F32)]
    return pl.pallas_call(
        functools.partial(windows_kernel, n_att, last),
        in_specs=[pl.BlockSpec(memory_space=pltpu.SMEM), vmem, vmem]
        + [pl.BlockSpec(memory_space=pltpu.HBM)] * 4
        + [vmem],
        out_specs=[vmem] * len(shapes),
        out_shape=shapes,
        scratch_shapes=[pltpu.VMEM((512, rows), F32)] * last
        + [pltpu.VMEM((v.shape[0], v.shape[1] // 2), BF) for v in blocks]
        + [pltpu.SemaphoreType.DMA((4,))],
        compiler_params=pltpu.CompilerParams(vmem_limit_bytes=24 << 20),
        cost_estimate=pl.CostEstimate(
            flops=rows * 512 * (b.shape[0] + a.shape[0]),
            bytes_accessed=8 << 20,
            transcendentals=0,
        ),
        name="windows",
    )(jnp.stack([core, lax.axis_index("y")]), b, a, *blocks, acc)


TILE = 512


def finish_kernel(tiles_att, me_ref, mine, other, lam_g, basis_out, att, mlp, out_att, out_mlp, whole, lifted):
    step = pl.program_id(0)

    @pl.when(step == 0)
    def _():
        half = mine.shape[3]
        me = me_ref[0]
        for y in range(mine.shape[0]):
            for hi in range(2):
                at = (y * 2 + hi) * 2 * half
                for l in range(2):
                    for c, ref in ((me, mine), (1 - me, other)):
                        rows = pl.ds(pl.multiple_of(at + c * half, half), half)
                        whole[l, rows, :] = ref[y, hi, l].astype(F32)
        for l in range(2):
            core = whole[l, :, :512]
            lam_a = jnp.sum(whole[l, :, 512:], axis=1, keepdims=True)
            gains = lam_g[l : l + 1, :]
            damp = DAMP_REL * jnp.mean(gains) * jnp.mean(lam_a)
            scaled = core / (gains * lam_a + damp)
            high = scaled.astype(BF)
            low = (scaled - high.astype(F32)).astype(BF)
            lifted[l] = (matmul_t(basis_out[l], high) + matmul_t(basis_out[l], low)).astype(BF)

    @pl.when(step < tiles_att)
    def _():
        out_att[...] = matmul_t(lifted[0], att[...]).astype(BF)

    @pl.when(step >= tiles_att)
    def _():
        out_mlp[...] = matmul_t(lifted[1], mlp[...]).astype(BF)


def finish(mine, other, lam_g, basis_out, att, mlp):
    rows = basis_out.shape[1]
    na, nm = att.shape[0] // TILE, mlp.shape[0] // TILE

    def at_att(i):
        return jnp.minimum(i, na - 1)

    def at_mlp(i):
        return jnp.maximum(i - na, 0)

    vmem = pl.BlockSpec(memory_space=pltpu.VMEM)
    return pl.pallas_call(
        functools.partial(finish_kernel, na),
        grid=(na + nm,),
        in_specs=[pl.BlockSpec(memory_space=pltpu.SMEM), vmem, vmem, vmem, vmem]
        + [
            pl.BlockSpec((TILE, 512), lambda i: (at_att(i), 0)),
            pl.BlockSpec((TILE, 512), lambda i: (at_mlp(i), 0)),
        ],
        out_specs=[
            pl.BlockSpec((rows, TILE), lambda i: (0, at_att(i))),
            pl.BlockSpec((rows, TILE), lambda i: (0, at_mlp(i))),
        ],
        out_shape=[
            jax.ShapeDtypeStruct((rows, att.shape[0]), BF),
            jax.ShapeDtypeStruct((rows, mlp.shape[0]), BF),
        ],
        scratch_shapes=[pltpu.VMEM((2, 512, 640), F32), pltpu.VMEM((2, rows, 512), BF)],
        compiler_params=pltpu.CompilerParams(vmem_limit_bytes=24 << 20),
        cost_estimate=pl.CostEstimate(
            flops=2 * rows * 512 * (att.shape[0] + mlp.shape[0]),
            bytes_accessed=8 << 20,
            transcendentals=0,
        ),
        name="finish",
    )(lax.axis_index("core")[None], mine, other, lam_g, basis_out, att, mlp)


def body(
    grad_att,
    grad_mlp,
    acts_att,
    acts_mlp,
    basis_in_att,
    basis_in_mlp,
    basis_out_att,
    basis_out_mlp,
    lam_out,
    owner_dp,
    owner_grad,
):
    rows = grad_att.shape[0]
    tokens_all = rows * 32
    out = jnp.stack(
        [
            jnp.concatenate(
                [v[0], jnp.stack(split3(lam_out[0, l])), jnp.zeros((29, 512), BF)], 0
            )
            for l, v in enumerate((basis_out_att, basis_out_mlp))
        ]
    )
    att, mlp, halves, out = broadcast(basis_in_att[0], basis_in_mlp[0], owner_dp, out, owner_grad)
    basis_out = out[:, :rows]
    lam_g = jnp.sum(out[:, rows : rows + 3].astype(F32), axis=1)

    me = lax.axis_index("core")
    blocks = (grad_att, acts_att, grad_mlp, acts_mlp)
    (acc,) = windows(me, halves[0], blocks, jnp.zeros((4 * rows, 512), F32), False)
    part, *sent = windows(1 - me, halves[1], blocks, acc, True)
    part = add_up(part, sent, "y")
    hi, half = lax.axis_index("z_hi"), part.shape[0] // 2
    part = add_up(block(part, hi, half), [block(part, 1 - hi, half).astype(BF)], "z_hi")

    mine = []
    for l in range(2):
        rot = part[:, 2 * l * rows : (2 * l + 1) * rows]
        proj = part[:, (2 * l + 1) * rows : (2 * l + 2) * rows]
        lam = jnp.sum(proj * proj, axis=1, keepdims=True) / tokens_all
        both = jnp.concatenate([v.astype(BF) for v in split2(rot)], 0)
        both = jnp.dot(both, basis_out[l], preferred_element_type=F32)
        n = rot.shape[0]
        mine.append((both[:n] + both[n:], lam))
    half = part.shape[0] // 2
    me = lax.axis_index("core")
    core = jnp.concatenate([block(c, me, half) for c, _ in mine], 0)
    lam = jnp.concatenate([block(e, me, half) for _, e in mine], 0)
    sent = packed(
        jnp.concatenate([block(c, 1 - me, half) for c, _ in mine], 0),
        jnp.concatenate([block(e, 1 - me, half) for _, e in mine], 0),
    )
    c, e = unpacked(swap(sent, "core"))
    core, lam = core + c, lam + e
    for axis in ("x", "z_lo"):
        sent = packed(core, lam)
        for v in [swap(sent, axis, k) for k in (1, 2, 3)]:
            c, e = unpacked(v)
            core, lam = core + c, lam + e

    wide = packed(core, lam).reshape(2, half, 640)
    wide = stack(stack(wide, "z_hi"), "y")
    (other,) = start((wide, "core", 1))
    return finish(wide, other, lam_g, basis_out, att, mlp)


def solution(mesh):
    fine = Mesh(mesh.devices.reshape(SIZES), AXES)
    placed = (
        P(DP, GRAD),
        P(DP, GRAD),
        P(DP, GRAD),
        P(DP, GRAD),
        P(DP, GRAD, None),
        P(DP, GRAD, None),
        P(GRAD, DP, None),
        P(GRAD, DP, None),
        P(GRAD, None, None),
        P(),
        P(),
    )
    return jax.shard_map(
        body,
        mesh=fine,
        in_specs=placed,
        out_specs=(P(DP, GRAD), P(DP, GRAD)),
        check_vma=False,
    )
```

```python
import functools

import jax
import jax.numpy as jnp
from jax import lax
from jax.experimental import pallas as pl
from jax.experimental.pallas import tpu as pltpu
from jax.sharding import Mesh, PartitionSpec as P

DAMP_REL = 0.1
AXES = ("z_lo", "x", "core", "z_hi", "y")
SIZES = (4, 4, 2, 2, 4)
SIZE = dict(zip(AXES, SIZES))
DP = ("z_lo", "x", "core")
GRAD = ("z_hi", "y")
BF = jnp.bfloat16
F32 = jnp.float32


def block(value, index, rows, axis=0):
    start = [0] * value.ndim
    start[axis] = index * rows
    size = list(value.shape)
    size[axis] = rows
    return lax.dynamic_slice(value, start, size, allow_negative_indices=False)


def put(value, part, index, axis=0):
    start = [0] * value.ndim
    start[axis] = index * part.shape[axis]
    return lax.dynamic_update_slice(value, part, start, allow_negative_indices=False)


def swap(value, axis, k=1):
    return lax.ppermute(value, axis, [(i, i ^ k) for i in range(SIZE[axis])])


def parts_out(value, axis):
    n, me = SIZE[axis], lax.axis_index(axis)
    return [(block(value, me ^ k, value.shape[1] // n, 1), axis, k) for k in range(1, n)]


def part_in(value, got, axis, at):
    n, me = SIZE[axis], lax.axis_index(axis)
    mine = block(value, me, value.shape[1] // n, 1)
    for k, g in enumerate(got, 1):
        mine = jnp.where(((me ^ k) == at).reshape(-1, 1, 1), g, mine)
    return mine


def all_out(value, axis):
    return [(value, axis, k) for k in range(1, SIZE[axis])]


def join(value, got, axis):
    n, me = SIZE[axis], lax.axis_index(axis)
    out = jnp.concatenate([value] * n, 1)
    for k, g in enumerate(got, 1):
        out = put(out, g, me ^ k, 1)
    return out


def start(*jobs, after=()):
    held = lax.optimization_barrier(tuple(job[0] for job in jobs) + tuple(after))
    return [swap(h, axis, k) for h, (_, axis, k) in zip(held, jobs)]


def split2(value):
    a = lax.reduce_precision(value, 8, 7)
    return a, lax.reduce_precision(value - a, 8, 7)


def split3(value):
    a, b = split2(value)
    return [a.astype(BF), b.astype(BF), (value - a - b).astype(BF)]


def packed(core, lam):
    a, b = split2(lam)
    lane = lax.broadcasted_iota(jnp.int32, (core.shape[0], 128), 1)
    more = jnp.where(lane == 0, a, jnp.where(lane == 1, b, 0.0))
    return jnp.concatenate([core.astype(BF), more.astype(BF)], 1)


def unpacked(value):
    wide = value.astype(F32)
    return wide[:, :512], jnp.sum(wide[:, 512:], axis=1, keepdims=True)


def matmul_t(a, b):
    return lax.dot_general(a, b, (((1,), (1,)), ((), ())), preferred_element_type=F32)


def broadcast(att, mlp, owner, out, owner_out):
    wide = att.shape[1]
    na, nm = att.shape[0] // 256, mlp.shape[0] // 256
    whole = jnp.concatenate([att.reshape(2, na, 128, wide), mlp.reshape(2, nm, 128, wide)], 1)
    cut = (na + nm) // 3
    at = jnp.concatenate([jnp.broadcast_to(owner[0], na), jnp.broadcast_to(owner[1], nm)])
    at_x, at_z = (at >> 1) & 3, at >> 3
    me = lax.axis_index("core")
    (got,) = start((block(whole, 1 - me, 1)[0], "core", 1))
    got_out = start(*parts_out(out, "y"))
    own = (me == (at & 1)).reshape(-1, 1, 1)
    value = jnp.where(own, block(whole, me, 1)[0], got)
    b, a = value[:cut], value[cut:]

    got = start(*parts_out(a, "x"), *parts_out(b, "z_lo"))
    a, b = part_in(a, got[:3], "x", at_x[cut:]), part_in(b, got[3:], "z_lo", at_z[:cut])
    out = part_in(out, got_out, "y", owner_out & 3)
    got = start(*parts_out(a, "z_lo"), *parts_out(b, "x"), (out, "z_hi", 1))
    a, b = part_in(a, got[:3], "z_lo", at_z[cut:]), part_in(b, got[3:6], "x", at_x[:cut])
    here = (lax.axis_index("z_hi") == (owner_out >> 2)).reshape(2, 1, 1)
    out = jnp.where(here, out, got[6])
    out_there = got[6:]

    got = start(*all_out(a, "z_lo"), *all_out(b, "x"))
    a, b = join(a, got[:3], "z_lo"), join(b, got[3:], "x")
    got = start(*all_out(a, "x"), *all_out(b, "z_lo"), after=out_there)
    a, b = join(a, got[:3], "x"), join(b, got[3:], "z_lo")
    other_b, other_a = start((b, "core", 1), (a, "core", 1))

    def whole_of(mine, other):
        return put(jnp.stack([mine, mine]), other[None], 1 - me)

    full_att = whole_of(b[:na], other_b[:na])
    full_mlp = whole_of(
        jnp.concatenate([b[na:], a], 0), jnp.concatenate([other_b[na:], other_a], 0)
    )
    halves = ((b, a), (other_b, other_a))
    return full_att.reshape(att.shape), full_mlp.reshape(mlp.shape), halves, out


def add_up(mine, sent, axis):
    got = [swap(v, axis, k) for k, v in enumerate(sent, 1)]
    return sum([g.astype(F32) for g in got], mine)


def stack(value, axis):
    n, me = SIZE[axis], lax.axis_index(axis)
    out = jnp.stack([value] * n)
    for k in range(1, n):
        out = put(out, swap(value, axis, k)[None], me ^ k)
    return out


def windows_kernel(n_att, last, at_ref, b, a, *refs):
    whole, acc = refs[:4], refs[4]
    outs = refs[5 : 9 if last else 6]
    turned, held, sems = refs[9 if last else 6] if last else None, refs[-5:-1], refs[-1]
    copies = []
    for i in range(4):
        n = held[i].shape[1]
        columns = pl.ds(pl.multiple_of(at_ref[0] * n, n), n)
        copies.append(pltpu.make_async_copy(whole[i].at[:, columns], held[i], sems.at[i]))
        copies[i].start()
    for i in range(4):
        g = held[i]
        rows = pl.ds(i * g.shape[0], g.shape[0])
        copies[i].wait()
        if i < 2:
            total = jnp.dot(g[...], b[:n_att, :], preferred_element_type=F32)
        else:
            n = b.shape[0] - n_att
            total = jnp.dot(g[:, :n], b[n_att:, :], preferred_element_type=F32)
            total += jnp.dot(g[:, n:], a[...], preferred_element_type=F32)
        total += acc[rows, :]
        if last:
            turned[:, rows] = total.T
        else:
            outs[0][rows, :] = total
    if last:
        n = outs[0].shape[0]
        for k, out in enumerate(outs):
            piece = at_ref[1] ^ k
            out[...] = turned[pl.ds(pl.multiple_of(piece * n, n), n), :].astype(out.dtype)


def windows(core, half, blocks, acc, last):
    b, a = (v.reshape(-1, v.shape[-1]) for v in half)
    n_att = blocks[0].shape[1] // 2
    rows = 4 * blocks[0].shape[0]
    vmem = pl.BlockSpec(memory_space=pltpu.VMEM)
    if last:
        shapes = [jax.ShapeDtypeStruct((128, rows), t) for t in (F32, BF, BF, BF)]
    else:
        shapes = [jax.ShapeDtypeStruct((rows, 512), F32)]
    return pl.pallas_call(
        functools.partial(windows_kernel, n_att, last),
        in_specs=[pl.BlockSpec(memory_space=pltpu.SMEM), vmem, vmem]
        + [pl.BlockSpec(memory_space=pltpu.HBM)] * 4
        + [vmem],
        out_specs=[vmem] * len(shapes),
        out_shape=shapes,
        scratch_shapes=[pltpu.VMEM((512, rows), F32)] * last
        + [pltpu.VMEM((v.shape[0], v.shape[1] // 2), BF) for v in blocks]
        + [pltpu.SemaphoreType.DMA((4,))],
        compiler_params=pltpu.CompilerParams(vmem_limit_bytes=24 << 20),
        cost_estimate=pl.CostEstimate(
            flops=rows * 512 * (b.shape[0] + a.shape[0]),
            bytes_accessed=8 << 20,
            transcendentals=0,
        ),
        name="windows",
    )(jnp.stack([core, lax.axis_index("y")]), b, a, *blocks, acc)


TILE = 512


def finish_kernel(tiles_att, me_ref, mine, other, lam_g, basis_out, att, mlp, out_att, out_mlp, whole, lifted):
    step = pl.program_id(0)

    @pl.when(step == 0)
    def _():
        half = mine.shape[3]
        me = me_ref[0]
        for y in range(mine.shape[0]):
            for hi in range(2):
                at = (y * 2 + hi) * 2 * half
                for l in range(2):
                    for c, ref in ((me, mine), (1 - me, other)):
                        rows = pl.ds(pl.multiple_of(at + c * half, half), half)
                        whole[l, rows, :] = ref[y, hi, l].astype(F32)
        for l in range(2):
            core = whole[l, :, :512]
            lam_a = jnp.sum(whole[l, :, 512:], axis=1, keepdims=True)
            gains = lam_g[l : l + 1, :]
            damp = DAMP_REL * jnp.mean(gains) * jnp.mean(lam_a)
            scaled = core / (gains * lam_a + damp)
            high = scaled.astype(BF)
            low = (scaled - high.astype(F32)).astype(BF)
            lifted[l] = (matmul_t(basis_out[l], high) + matmul_t(basis_out[l], low)).astype(BF)

    @pl.when(step < tiles_att)
    def _():
        out_att[...] = matmul_t(lifted[0], att[...]).astype(BF)

    @pl.when(step >= tiles_att)
    def _():
        out_mlp[...] = matmul_t(lifted[1], mlp[...]).astype(BF)


def finish(mine, other, lam_g, basis_out, att, mlp):
    rows = basis_out.shape[1]
    na, nm = att.shape[0] // TILE, mlp.shape[0] // TILE

    def at_att(i):
        return jnp.minimum(i, na - 1)

    def at_mlp(i):
        return jnp.maximum(i - na, 0)

    vmem = pl.BlockSpec(memory_space=pltpu.VMEM)
    return pl.pallas_call(
        functools.partial(finish_kernel, na),
        grid=(na + nm,),
        in_specs=[pl.BlockSpec(memory_space=pltpu.SMEM), vmem, vmem, vmem, vmem]
        + [
            pl.BlockSpec((TILE, 512), lambda i: (at_att(i), 0)),
            pl.BlockSpec((TILE, 512), lambda i: (at_mlp(i), 0)),
        ],
        out_specs=[
            pl.BlockSpec((rows, TILE), lambda i: (0, at_att(i))),
            pl.BlockSpec((rows, TILE), lambda i: (0, at_mlp(i))),
        ],
        out_shape=[
            jax.ShapeDtypeStruct((rows, att.shape[0]), BF),
            jax.ShapeDtypeStruct((rows, mlp.shape[0]), BF),
        ],
        scratch_shapes=[pltpu.VMEM((2, 512, 640), F32), pltpu.VMEM((2, rows, 512), BF)],
        compiler_params=pltpu.CompilerParams(vmem_limit_bytes=24 << 20),
        cost_estimate=pl.CostEstimate(
            flops=2 * rows * 512 * (att.shape[0] + mlp.shape[0]),
            bytes_accessed=8 << 20,
            transcendentals=0,
        ),
        name="finish",
    )(lax.axis_index("core")[None], mine, other, lam_g, basis_out, att, mlp)


def body(
    grad_att,
    grad_mlp,
    acts_att,
    acts_mlp,
    basis_in_att,
    basis_in_mlp,
    basis_out_att,
    basis_out_mlp,
    lam_out,
    owner_dp,
    owner_grad,
):
    rows = grad_att.shape[0]
    tokens_all = rows * 32
    out = jnp.stack(
        [
            jnp.concatenate(
                [v[0], jnp.stack(split3(lam_out[0, l])), jnp.zeros((29, 512), BF)], 0
            )
            for l, v in enumerate((basis_out_att, basis_out_mlp))
        ]
    )
    att, mlp, halves, out = broadcast(basis_in_att[0], basis_in_mlp[0], owner_dp, out, owner_grad)
    me = lax.axis_index("core")
    blocks = (grad_att, acts_att, grad_mlp, acts_mlp)
    (acc,) = windows(me, halves[0], blocks, jnp.zeros((4 * rows, 512), F32), False)
    part, *sent = windows(1 - me, halves[1], blocks, acc, True)
    part = add_up(part, sent, "y")
    hi, half = lax.axis_index("z_hi"), part.shape[0] // 2
    other, *got = start((block(part, 1 - hi, half).astype(BF), "z_hi", 1), *all_out(out, "y"))
    part = block(part, hi, half) + other.astype(F32)
    out = join(out, got, "y")
    basis_out = out[:, :rows]
    lam_g = jnp.sum(out[:, rows : rows + 3].astype(F32), axis=1)

    mine = []
    for l in range(2):
        rot = part[:, 2 * l * rows : (2 * l + 1) * rows]
        proj = part[:, (2 * l + 1) * rows : (2 * l + 2) * rows]
        lam = jnp.sum(proj * proj, axis=1, keepdims=True) / tokens_all
        both = jnp.concatenate([v.astype(BF) for v in split2(rot)], 0)
        both = jnp.dot(both, basis_out[l], preferred_element_type=F32)
        n = rot.shape[0]
        mine.append((both[:n] + both[n:], lam))
    half = part.shape[0] // 2
    me = lax.axis_index("core")
    core = jnp.concatenate([block(c, me, half) for c, _ in mine], 0)
    lam = jnp.concatenate([block(e, me, half) for _, e in mine], 0)
    sent = packed(
        jnp.concatenate([block(c, 1 - me, half) for c, _ in mine], 0),
        jnp.concatenate([block(e, 1 - me, half) for _, e in mine], 0),
    )
    c, e = unpacked(swap(sent, "core"))
    core, lam = core + c, lam + e
    for axis in ("x", "z_lo"):
        sent = packed(core, lam)
        for v in [swap(sent, axis, k) for k in (1, 2, 3)]:
            c, e = unpacked(v)
            core, lam = core + c, lam + e

    wide = packed(core, lam).reshape(2, half, 640)
    wide = stack(stack(wide, "z_hi"), "y")
    (other,) = start((wide, "core", 1))
    return finish(wide, other, lam_g, basis_out, att, mlp)


def solution(mesh):
    fine = Mesh(mesh.devices.reshape(SIZES), AXES)
    placed = (
        P(DP, GRAD),
        P(DP, GRAD),
        P(DP, GRAD),
        P(DP, GRAD),
        P(DP, GRAD, None),
        P(DP, GRAD, None),
        P(GRAD, DP, None),
        P(GRAD, DP, None),
        P(GRAD, None, None),
        P(),
        P(),
    )
    return jax.shard_map(
        body,
        mesh=fine,
        in_specs=placed,
        out_specs=(P(DP, GRAD), P(DP, GRAD)),
        check_vma=False,
    )
```
